32 devices in a mesh: dp: 8 (over z, x), tensor: 4 (over y, core).
Axes of the slice: x: 2, y: 2, z: 4, core: 2. Of those that a mesh axis runs over, the one named last changes fastest.
Arguments:
- block_input: float32 [18912, 768], P(('dp', 'tensor')), may hold values from -6 to 6
- cotangent: float32 [18912, 768], P(('dp', 'tensor')), may hold values from -6 to 6
- query_weight: float32 [768, 768], P('dp', 'tensor'), may hold values from -0.21875 to 0.21875
- key_weight: float32 [768, 768], P('dp', 'tensor'), may hold values from -0.21875 to 0.21875
- value_weight: float32 [768, 768], P('dp', 'tensor'), may hold values from -0.21875 to 0.21875
- output_weight: float32 [768, 768], P('tensor', 'dp'), may hold values from -1.75 to 1.75
- first_gain: float32 [768], P('dp'), may hold values from 0.5 to 1.5
- first_shift: float32 [768], P('dp'), may hold values from -1 to 1
- expert_in: float32 [8, 768, 3072], P(None, 'dp', 'tensor'), may hold values from -0.21875 to 0.21875
- expert_out: float32 [8, 3072, 768], P(None, 'tensor', 'dp'), may hold values from -0.21875 to 0.21875
- second_gain: float32 [768], P('dp'), may hold values from 0.5 to 1.5
- second_shift: float32 [768], P('dp'), may hold values from -1 to 1
- routes: int32 [18912, 2], P('dp'), may hold values from 0 to 7, all different within a row; in each aligned block of 2364 rows (0 to 2363, 2364 to 4727, ...) at most 792 rows name the same one
- route_gates: float32 [18912, 2], P('dp'), may hold values from 0.25 to 0.75
- clip_threshold: float32 [12], P('tensor'), may hold values from 3 to 9
Outputs:
- block_output: float32 [18912, 768], P(('dp', 'tensor'))
- input_grad: float32 [18912, 768], P(('dp', 'tensor'))
- query_grad: float32 [768, 768], P('dp', 'tensor')
- key_grad: float32 [768, 768], P('dp', 'tensor')
- value_grad: float32 [768, 768], P('dp', 'tensor')
- output_grad: float32 [768, 768], P('tensor', 'dp')
- first_gain_grad: float32 [768], P('dp')
- first_shift_grad: float32 [768], P('dp')
- expert_in_grad: float32 [8, 768, 3072], P(None, 'dp', 'tensor')
- expert_out_grad: float32 [8, 3072, 768], P(None, 'tensor', 'dp')
- second_gain_grad: float32 [768], P('dp')
- second_shift_grad: float32 [768], P('dp')
- clipped_query: float32 [768, 768], P('dp', 'tensor')
- clipped_key: float32 [768, 768], P('dp', 'tensor')
- head_maxima: float32 [12], P('tensor')
The draws below stay inside these ranges and needn't reach their ends.
Inputs may be any that keep to these rules, and one draw needn't show every extreme that they name: `routes`: each row names two different experts. In each aligned block of 2364 rows (the tokens of one index of dp) no expert is named by more than 792 rows, a bound that some block reaches.
All inputs are finite; a program needn't handle non-finite values.
Results may differ from the reference program's by a relative error of at most 0.018.
Values may be sent and summed in bfloat16 or wider, within the bound.
No kernel may reach another device: no remote copies, remote signals or barrier semaphores. Data moves between devices by JAX's collectives and lax.ppermute only.
A program may use at most 320 MiB of HBM per device.

```python
import math
import jax
import jax.numpy as jnp
import numpy as np
from jax import lax

D = 768
HEADS = 12
HD = 64
FF = 3072
EXPERTS = 8
SEQ = 197
GROUP_TOK = 2364
TOKENS = 18912
CAP = 792


def level_of(key, shape, cuts, low, top_value):
    gain = 1.0
    for dim, blocks in cuts:
        heights = jax.random.uniform(jax.random.fold_in(jax.random.fold_in(key, 6), dim), (blocks,), jnp.float32, low / len(cuts), top_value / len(cuts))
        gain = gain * jnp.repeat(jnp.exp(heights), shape[dim] // blocks).reshape((-1,) + (1,) * (len(shape) - 1 - dim))
    return gain


def deal_out(rng, own, number, rows, count, top, bound, lean):
    order = jax.random.permutation(rng, count)
    heavy_load, usual = load_shares(count, rows * top, bound, lean, True), load_shares(count, rows * top, bound, lean, False)
    places = jnp.arange(count)

    def named(sizes, rotation):
        used = int((sizes > 0).sum())
        fixed = max(1, used // 4)
        moved = fixed + (places - fixed + rotation * (used - fixed)) % max(1, count - fixed)
        return jnp.zeros((count,), jnp.int32).at[order[jnp.where(places < fixed, places, moved)]].set(jnp.asarray(sizes, jnp.int32))

    sizes = jnp.where(number % 4 == 0, named(heavy_load, number // 4), named(usual, number - number // 4 - 1))
    mixed = jax.random.permutation(jax.random.fold_in(own, 3), count)
    source_of, receiver = mixed[0:count // 2 * 2:2], mixed[1:count // 2 * 2:2]
    room = jnp.minimum(sizes[source_of] - 1, bound - sizes[receiver]) // 2
    room = jnp.where((source_of == order[0]) | (receiver == order[0]) | (sizes[receiver] == 0), 0, jnp.maximum(room, 0))
    moved = jax.random.randint(jax.random.fold_in(own, 4), (count // 2,), 0, 1 << 20) % (room + 1)
    sizes = sizes.at[source_of].add(-moved).at[receiver].add(moved)
    members = jnp.searchsorted(jnp.cumsum(sizes), jnp.arange(rows * top), side="right").astype(jnp.int32)
    table = members.reshape(top, rows).T
    table = table[jax.random.permutation(jax.random.fold_in(own, 1), rows)]
    rotation = jax.random.randint(jax.random.fold_in(own, 2), (rows, 1), 0, top)
    return jnp.take_along_axis(table, (jnp.arange(top)[None, :] + rotation) % top, axis=1)


def load_shares(number_of, total, bound, slope, full):
    weights = [(1 << 20) // math.isqrt(grade ** slope) + 1 for grade in range(1, number_of + 1)]
    largest = bound if full else min(bound, max(-(-total // number_of), total * weights[0] // sum(weights)))
    least = 1 if total - largest >= number_of - 1 else 0
    holding, rest = [largest] + [least] * (number_of - 1), total - largest - least * (number_of - 1)
    while rest > 0:
        free = [i for i in range(1, number_of) if holding[i] < largest] or [i for i in range(1, number_of) if holding[i] < bound]
        whole, left = sum([weights[i] for i in free]), rest
        for i in free:
            more = min(bound - holding[i], max(1, left * weights[i] // whole), rest)
            holding[i] = holding[i] + more
            rest = rest - more
    return np.array(holding)


def noise(rng, shape, deviation, reach, shards=(), dtype=jnp.bfloat16):
    loudness = level_of(rng, shape, shards, -0.22, 0.18) if shards else 1.0
    entries = jax.random.normal(rng, shape, jnp.float32) * deviation * loudness
    return jnp.minimum(jnp.maximum(entries, -reach), reach).astype(dtype)


def setup_inputs(seed: int = 0) -> dict:
    key_of = jax.random.split(jax.random.key(seed), 16)
    block_input = noise(key_of[0], (TOKENS, D), 1.0, 6.0, ((0, 32),), jnp.float32)
    cotangent = noise(key_of[1], (TOKENS, D), 1.0, 6.0, ((0, 32),), jnp.float32)
    query_weight = noise(key_of[2], (D, D), D ** -0.5, 0.21875, ((0, 8), (1, 4)), jnp.float32)
    key_weight = noise(key_of[3], (D, D), D ** -0.5, 0.21875, ((0, 8), (1, 4)), jnp.float32)
    value_weight = noise(key_of[4], (D, D), D ** -0.5, 0.21875, ((0, 8), (1, 4)), jnp.float32)
    output_weight = noise(key_of[5], (D, D), (D // 64) ** -0.5, 1.75, ((0, 4), (1, 8)), jnp.float32)
    first_gain = jnp.clip(1.0 + 0.1 * jax.random.normal(key_of[6], (D,), jnp.float32), 0.5, 1.5)
    first_shift = noise(key_of[7], (D,), 0.2, 1.0, ((0, 8),), jnp.float32)
    expert_in = noise(key_of[8], (EXPERTS, D, FF), D ** -0.5, 0.21875, ((1, 8), (2, 4)), jnp.float32)
    expert_out = noise(key_of[9], (EXPERTS, FF, D), (FF // 4) ** -0.5, 0.21875, ((1, 4), (2, 8)), jnp.float32)
    second_gain = jnp.clip(1.0 + 0.1 * jax.random.normal(key_of[10], (D,), jnp.float32), 0.5, 1.5)
    second_shift = noise(key_of[11], (D,), 0.2, 1.0, ((0, 8),), jnp.float32)
    routes_keys = jax.random.split(jax.random.fold_in(key_of[12], 1), TOKENS // GROUP_TOK)
    routes_turns = jax.random.permutation(jax.random.fold_in(key_of[12], 3), TOKENS // GROUP_TOK)
    routes = jax.vmap(lambda own, number: deal_out(jax.random.fold_in(key_of[12], 2), own, number, GROUP_TOK, EXPERTS, 2, CAP, 1))(routes_keys, routes_turns).reshape((TOKENS, 2))
    route_gates = jnp.clip(0.25 + 0.5 * jax.random.uniform(key_of[13], (TOKENS, 2), jnp.float32) ** level_of(key_of[13], (TOKENS, 2), ((0, 8),), -0.2, 0.2), 0.25, 0.75)
    clip_threshold = jnp.clip(3.0 + 6.0 * jax.random.uniform(key_of[14], (HEADS,), jnp.float32) ** level_of(key_of[14], (HEADS,), ((0, 4),), -0.2, 0.2), 3.0, 9.0)
    return {"block_input": block_input, "cotangent": cotangent, "query_weight": query_weight, "key_weight": key_weight, "value_weight": value_weight, "output_weight": output_weight, "first_gain": first_gain, "first_shift": first_shift, "expert_in": expert_in, "expert_out": expert_out, "second_gain": second_gain, "second_shift": second_shift, "routes": routes, "route_gates": route_gates, "clip_threshold": clip_threshold}


EPSILON = 1e-06
PRECISE = lax.Precision.HIGHEST

@jax.custom_vjp
def low(v):
    return lax.optimization_barrier(v.astype(jnp.bfloat16)).astype(jnp.float32)

@jax.custom_vjp
def low_back(v):
    return v

def low_keep(v):
    return (low(v), None)

def low_pass(kept, grad):
    return (grad,)

def back_keep(v):
    return (v, None)

def back_low(kept, grad):
    return (low(grad),)
low.defvjp(low_keep, low_pass)
low_back.defvjp(back_keep, back_low)

def layer_norm(values, gain_row, shift_row):
    row_mean = lax.optimization_barrier(jnp.mean(values, -1, keepdims=True))
    centred = values - row_mean
    spread = lax.optimization_barrier(jnp.mean(centred * centred, -1, keepdims=True))
    return centred * lax.rsqrt(spread + EPSILON) * gain_row + shift_row

def matmul(left, right):
    return jnp.dot(left, right, precision=PRECISE, preferred_element_type=jnp.float32)

def group_forward(params, row_block, route_ids, gate_block):
    w_query, w_key, w_value, w_output, gain_one, shift_one, w_in, w_down, gain_two, shift_two = params
    image_count = row_block.shape[0] // SEQ
    score_scale = 1.0 / math.sqrt(HD)
    normed = low(layer_norm(row_block, gain_one, shift_one))
    query_heads = low_back(low(matmul(normed, w_query))).reshape(image_count, SEQ, HEADS, HD)
    key_heads = low_back(low(matmul(normed, w_key))).reshape(image_count, SEQ, HEADS, HD)
    value_heads = low_back(low(matmul(normed, w_value))).reshape(image_count, SEQ, HEADS, HD)
    scores = low_back(jnp.einsum('ishd,ithd->ihst', query_heads, key_heads, precision=PRECISE) * score_scale)
    peak_block = lax.optimization_barrier(jnp.max(scores, axis=(0, 2, 3)))
    row_top = lax.optimization_barrier(jnp.max(scores, -1, keepdims=True))
    exponent = jnp.exp(scores - row_top)
    attention = exponent / lax.optimization_barrier(jnp.sum(exponent, -1, keepdims=True))
    mixed_heads = jnp.einsum('ihst,ithd->ishd', low(attention), value_heads, precision=PRECISE)
    mixed_heads = low_back(low(mixed_heads.reshape(row_block.shape[0], HEADS * HD)))
    attended = low_back(matmul(mixed_heads, w_output))
    residual = row_block + attended
    normed_two = low(layer_norm(residual, gain_two, shift_two))
    mixture = jnp.zeros_like(row_block)
    for expert_index in range(EXPERTS):
        weight = lax.optimization_barrier(jnp.sum(jnp.where(route_ids == expert_index, gate_block, jnp.zeros_like(gate_block)), -1))
        hidden_pre = low_back(matmul(normed_two, w_in[expert_index]))
        activated = low(jax.nn.gelu(hidden_pre, approximate=False))
        mixture = mixture + weight[:, None] * low_back(matmul(activated, w_down[expert_index]))
    return (residual + low_back(mixture), peak_block)

def reference(block_input, cotangent, query_weight, key_weight, value_weight, output_weight, first_gain, first_shift, expert_in, expert_out, second_gain, second_shift, routes, route_gates, clip_threshold):
    groups = block_input.shape[0] // GROUP_TOK
    picks = routes.shape[1]
    route_blocks = routes.reshape(groups, GROUP_TOK, picks)
    gate_blocks = route_gates.reshape(groups, GROUP_TOK, picks)

    def forward(w_query, w_key, w_value, w_output, gain_one, shift_one, w_in, w_down, gain_two, shift_two, rows_all):
        params = tuple((low(weight) for weight in (w_query, w_key, w_value, w_output, gain_one, shift_one, w_in, w_down, gain_two, shift_two)))

        def scan_step(scan_carry, pieces):
            return (scan_carry, group_forward(params, pieces[0], pieces[1], pieces[2]))
        _, (outputs, peaks) = lax.scan(jax.checkpoint(scan_step), jnp.zeros((), jnp.float32), (rows_all.reshape(groups, GROUP_TOK, D), route_blocks, gate_blocks))
        return (outputs.reshape(groups * GROUP_TOK, D), peaks)
    (block_output, peaks), pullback = jax.vjp(forward, query_weight, key_weight, value_weight, output_weight, first_gain, first_shift, expert_in, expert_out, second_gain, second_shift, block_input)
    grads = pullback((cotangent, jnp.zeros_like(peaks)))
    head_maxima = lax.optimization_barrier(jnp.max(peaks, 0))
    factor = jnp.minimum(1.0, clip_threshold / jnp.maximum(head_maxima, 1.0))
    column_scale = jnp.repeat(jnp.sqrt(factor), HD)
    return (block_output, grads[10], grads[0], grads[1], grads[2], grads[3], grads[4], grads[5], grads[6], grads[7], grads[8], grads[9], query_weight * column_scale[None, :], key_weight * column_scale[None, :], head_maxima)
```

```python
import functools
import math

import jax
import jax.numpy as jnp
from jax import lax
from jax.experimental import pallas as pl
from jax.experimental.pallas import tpu as pltpu
from jax.sharding import PartitionSpec as P

HD = 64
SEQ = 197
CAP = 792
EPSILON = 1e-06
F32 = jnp.float32
BF16 = jnp.bfloat16
OUTER = 8
EXTRA = 16
ROW_TILE = 400
WINDOW = 256
MIB = 1 << 20


def up(number, unit):
    return -(-number // unit) * unit


def dot(left, right, contract=((1,), (0,))):
    return lax.dot_general(left, right, (contract, ((), ())), preferred_element_type=F32)


def params(mib):
    return pltpu.CompilerParams(vmem_limit_bytes=mib * MIB)


def any_spec():
    return pl.BlockSpec(memory_space=pl.ANY)


def vmem_spec():
    return pl.BlockSpec(memory_space=pltpu.VMEM)


def smem_spec():
    return pl.BlockSpec(memory_space=pltpu.SMEM)


def sds(shape, dtype):
    return jax.ShapeDtypeStruct(shape, dtype)


def cost(flops, moved, trans=0):
    return pl.CostEstimate(flops=int(flops), bytes_accessed=int(moved), transcendentals=int(trans))


def block_flip(x_bit, low_bit, high_bit):
    return x_bit | low_bit << 1 | high_bit << 2


def norm_stats(values):
    mean = jnp.mean(values, -1, keepdims=True)
    centred = values - mean
    scale = lax.rsqrt(jnp.mean(centred * centred, -1, keepdims=True) + EPSILON)
    return centred * scale, scale


def spread_rows(source, target, images, stride):
    for i in range(images):
        target[i * stride : i * stride + SEQ, :] = source[i * SEQ : (i + 1) * SEQ, :].astype(F32)
        end = (i + 1) * stride if i + 1 < images else target.shape[0]
        target[i * stride + SEQ : end, :] = jnp.zeros((end - i * stride - SEQ, target.shape[1]), F32)


def gather_rows(source, target, images, stride):
    for i in range(images):
        target[i * SEQ : (i + 1) * SEQ, :] = source[i * stride : i * stride + SEQ, :]


def attention_forward_kernel(images, stride, heads, layout, *refs):
    n_pieces = len(layout)
    place_ref, x_ref, gains_ref = refs[:3]
    piece_refs = refs[3 : 3 + n_pieces]
    res_ref, second_ref, first_ref, w_ref, kept_ref, peak_ref = refs[3 + n_pieces : 9 + n_pieces]
    scratch, sems = refs[9 + n_pieces :]
    columns = heads * HD
    block = w_ref.shape[1] // OUTER
    place = place_ref[0]
    copies = []
    for ref, entries in zip(piece_refs, layout):
        for j, (t, flip) in enumerate(entries):
            row = pl.multiple_of((place ^ flip) * block, 16)
            copies.append(
                pltpu.make_async_copy(
                    ref.at[j, pl.ds(0, block), :],
                    w_ref.at[t, pl.ds(row, block), :],
                    sems.at[len(copies)],
                )
            )
            copies[-1].start()
    spread_rows(x_ref, res_ref, images, stride)
    unit, _ = norm_stats(res_ref[...])
    first_ref[...] = (unit * gains_ref[0:1, :] + gains_ref[1:2, :]).astype(BF16)
    for copy in copies:
        copy.wait()
    scale = 1.0 / math.sqrt(HD)
    col_ok = lax.broadcasted_iota(jnp.int32, (stride, stride), 1) < SEQ
    row_ok = lax.broadcasted_iota(jnp.int32, (stride, 1), 0) < SEQ
    lane = lax.broadcasted_iota(jnp.int32, (8, 128), 1)

    def step(t, carry):
        scratch[...] = dot(first_ref[...], w_ref[t]).astype(BF16).astype(F32)
        peaks = jnp.full((8, 128), -jnp.inf, F32)
        for i in range(images):
            rows = slice(i * stride, (i + 1) * stride)
            for h in range(heads):
                at = [slice((1 + p) * columns + h * HD, (1 + p) * columns + (h + 1) * HD) for p in range(3)]
                q = (scratch[rows, at[0]] * scale).astype(BF16)
                k = scratch[rows, at[1]].astype(BF16)
                v = scratch[rows, at[2]].astype(BF16)
                s = jnp.where(col_ok, dot(q, k, ((1,), (1,))), -1e30)
                top = jnp.max(s, -1, keepdims=True)
                e = jnp.exp(s - top)
                p = e * (1.0 / jnp.sum(e, -1, keepdims=True))
                o = dot(p.astype(BF16), v)
                scratch[rows, h * HD : (h + 1) * HD] = o.astype(BF16).astype(F32)
                peak = jnp.max(jnp.where(row_ok, top, -jnp.inf), keepdims=True)
                peaks = jnp.maximum(peaks, jnp.where(lane == h, peak, -jnp.inf))
        peak_ref[t] = peaks
        kept_ref[t] = scratch[...].astype(BF16)
        res_ref[...] += dot(kept_ref[t, :, 0:columns], w_ref[t, :, 0:columns], ((1,), (1,)))
        return carry

    lax.fori_loop(0, w_ref.shape[0], step, 0)
    unit, _ = norm_stats(res_ref[...])
    second_ref[...] = (unit * gains_ref[2:3, :] + gains_ref[3:4, :]).astype(BF16)


def attention_forward(place, rows, gains, pieces, layout, images, stride, padded, parts, heads):
    features = rows.shape[1]
    n_copies = sum(len(entries) for entries in layout)
    return pl.pallas_call(
        functools.partial(attention_forward_kernel, images, stride, heads, layout),
        out_shape=(
            sds((padded, features), F32),
            sds((padded, features), BF16),
            sds((padded, features), BF16),
            sds((parts, features, features), BF16),
            sds((parts, padded, features), BF16),
            sds((parts, 8, 128), F32),
        ),
        in_specs=[smem_spec(), vmem_spec(), vmem_spec()] + [any_spec()] * len(pieces),
        out_specs=(vmem_spec(),) * 6,
        scratch_shapes=[
            pltpu.VMEM((padded, features), F32),
            pltpu.SemaphoreType.DMA((n_copies,)),
        ],
        compiler_params=params(48),
        cost_estimate=cost(parts * padded * features * features * 2.6 * 4, 20e6, 2e6),
        name="attention_forward",
    )(place, rows, gains, *pieces)


def attention_backward_kernel(images, stride, heads, *refs):
    (x_ref, cot_ref, res_ref, d0_ref, d1_ref, d2_ref, first_ref, w_ref, kept_ref, gains_ref, extra_ref) = refs[:11]
    input_grad_ref, keep_ref, send_ref = refs[11:14]
    resid, total, kept, grads, mixed, half = refs[14:]
    columns = heads * HD
    parts = w_ref.shape[0]
    features = w_ref.shape[1]
    block = features // OUTER
    unit, scale_two = norm_stats(res_ref[...])
    da2 = d0_ref[...].astype(F32) + d1_ref[...].astype(F32) + d2_ref[...].astype(F32)
    gain_two = jnp.sum(da2 * unit, 0, keepdims=True)
    shift_two = jnp.sum(da2, 0, keepdims=True)
    weighted = da2 * gains_ref[2:3, :]
    back = (
        weighted
        - jnp.mean(weighted, -1, keepdims=True)
        - unit * jnp.mean(weighted * unit, -1, keepdims=True)
    ) * scale_two
    spread_rows(cot_ref, resid, images, stride)
    resid[...] += back
    half[...] = resid[...].astype(BF16)
    total[...] = jnp.zeros_like(total)
    grads[...] = jnp.zeros_like(grads)
    scale = 1.0 / math.sqrt(HD)
    col_ok = lax.broadcasted_iota(jnp.int32, (stride, stride), 1) < SEQ

    def step(t, carry):
        kept[...] = kept_ref[t].astype(F32)
        mixed[...] = dot(half[...], w_ref[t, :, 0:columns]).astype(BF16).astype(F32)
        for i in range(images):
            rows = slice(i * stride, (i + 1) * stride)
            for h in range(heads):
                at = [slice((1 + p) * columns + h * HD, (1 + p) * columns + (h + 1) * HD) for p in range(3)]
                q = (kept[rows, at[0]] * scale).astype(BF16)
                k = kept[rows, at[1]].astype(BF16)
                v = kept[rows, at[2]].astype(BF16)
                do = mixed[rows, h * HD : (h + 1) * HD].astype(BF16)
                s = jnp.where(col_ok, dot(q, k, ((1,), (1,))), -1e30)
                e = jnp.exp(s - jnp.max(s, -1, keepdims=True))
                p = e * (1.0 / jnp.sum(e, -1, keepdims=True))
                dp = dot(do, v, ((1,), (1,)))
                dv = dot(p.astype(BF16), do, ((0,), (0,)))
                ds = (p * (dp - jnp.sum(p * dp, -1, keepdims=True))).astype(BF16)
                dq = dot(ds, k) * scale
                dk = dot(ds, q, ((0,), (0,)))
                grads[rows, at[0]] = dq
                grads[rows, at[1]] = dk
                grads[rows, at[2]] = dv
        packed = grads[...].astype(BF16)
        total[...] += dot(packed, w_ref[t], ((1,), (1,)))
        full = dot(first_ref[...], packed, ((0,), (0,)))
        out = dot(half[...], kept_ref[t, :, 0:columns], ((0,), (0,)))
        full = full + jnp.concatenate((out, jnp.zeros((features, features - columns), F32)), 1)
        full = full.astype(BF16)

        def put(ref, index):
            for j in range(OUTER):
                ref[index, j, 0:block, :] = full[j * block : (j + 1) * block, :]

        @pl.when(t < parts // 2)
        def _():
            put(keep_ref, t)

        @pl.when(t >= parts // 2)
        def _():
            put(send_ref, t - parts // 2)

        return carry

    lax.fori_loop(0, parts, step, 0)
    spread_rows(x_ref, kept, images, stride)
    unit, scale_one = norm_stats(kept[...])
    da = total[...]
    gain_one = jnp.sum(da * unit, 0, keepdims=True)
    shift_one = jnp.sum(da, 0, keepdims=True)
    weighted = da * gains_ref[0:1, :]
    back = (
        weighted
        - jnp.mean(weighted, -1, keepdims=True)
        - unit * jnp.mean(weighted * unit, -1, keepdims=True)
    ) * scale_one
    resid[...] += back
    gather_rows(resid, input_grad_ref, images, stride)
    row = lax.broadcasted_iota(jnp.int32, (EXTRA, features), 0)
    extra = extra_ref[...]
    for number, value in enumerate((gain_one, shift_one, gain_two, shift_two)):
        extra = jnp.where(row == number, value, extra)
    extra = extra.astype(BF16)
    for ref in (keep_ref, send_ref):
        for t in range(parts // 2):
            for j in range(OUTER):
                ref[t, j, block : block + EXTRA, :] = extra


def attention_backward(rows, cot, residual, pieces, first, weights, kept, gains, extra, images, stride, heads):
    padded, features = first.shape
    parts = weights.shape[0]
    share = sds((parts // 2, OUTER, features // OUTER + EXTRA, features), BF16)
    return pl.pallas_call(
        functools.partial(attention_backward_kernel, images, stride, heads),
        out_shape=(sds(rows.shape, F32), share, share),
        in_specs=[vmem_spec()] * 11,
        out_specs=(vmem_spec(),) * 3,
        scratch_shapes=[
            pltpu.VMEM((padded, features), F32),
            pltpu.VMEM((padded, features), F32),
            pltpu.VMEM((padded, features), F32),
            pltpu.VMEM((padded, features), F32),
            pltpu.VMEM((padded, heads * HD), F32),
            pltpu.VMEM((padded, features), BF16),
        ],
        compiler_params=params(56),
        cost_estimate=cost(parts * padded * features * features * 2 * 4, 30e6, 2e6),
        name="attention_backward",
    )(rows, cot, residual, *pieces, first, weights, kept, gains, extra)


def dispatch_kernel(gated, *refs):
    table_ref = refs[0]
    n_shards = 8
    shard_refs = refs[1 : 1 + n_shards]
    slot_ref = refs[1 + n_shards]
    gate_ref = refs[2 + n_shards] if gated else None
    out_ref = refs[-1]
    expert = pl.program_id(0)
    experts = pl.num_programs(0)
    padded = shard_refs[0].shape[0]
    features = shard_refs[0].shape[1]
    count_all = table_ref[2 * n_shards * experts + expert]
    tail = pl.multiple_of(count_all // 16 * 16, 16)
    out_ref[0, pl.ds(tail, ROW_TILE + 16), :] = jnp.zeros((ROW_TILE + 16, features), BF16)
    row16 = lax.broadcasted_iota(jnp.int32, (16, 1), 0)
    rows = lax.broadcasted_iota(jnp.int32, (WINDOW, padded), 0)
    for r in range(n_shards):
        start = table_ref[expert * n_shards + r]
        number = table_ref[n_shards * experts + expert * n_shards + r]
        first = start // 16 * 16
        steps = jnp.where(number > 0, (start - first + number + WINDOW - 1) // WINDOW, 0)

        def step(c, carry, r=r, start=start, first=first):
            low = pl.multiple_of(first + c * WINDOW, 16)
            hit = slot_ref[0, r : r + 1, :] == rows + low
            chosen = jnp.where(hit, 1.0, 0.0)
            got = dot(chosen.astype(BF16), shard_refs[r][...])
            if gated:
                got = got * jnp.sum(chosen * gate_ref[0, r : r + 1, :], -1, keepdims=True)
            got = got.astype(BF16)
            before = out_ref[0, pl.ds(low, 16), :]
            out_ref[0, pl.ds(low, 16), :] = jnp.where(row16 + low < start, before, got[:16])
            out_ref[0, pl.ds(low + 16, WINDOW - 16), :] = got[16:]
            return carry

        lax.fori_loop(0, steps, step, 0)


def slot_rows(limit):
    return up(limit + ROW_TILE, 16) + up(ROW_TILE, 16)


def dispatch(table, shards, slots, gates, limit):
    experts = slots.shape[0]
    padded, features = shards[0].shape
    length = slot_rows(limit)
    gated = gates is not None
    per_expert = pl.BlockSpec((1,) + slots.shape[1:], lambda e: (e, 0, 0))
    return pl.pallas_call(
        functools.partial(dispatch_kernel, gated),
        grid=(experts,),
        out_shape=sds((experts, length, features), BF16),
        in_specs=[smem_spec()] + [vmem_spec()] * len(shards) + [per_expert] * (2 if gated else 1),
        out_specs=pl.BlockSpec((1, length, features), lambda e: (e, 0, 0)),
        compiler_params=params(48),
        cost_estimate=cost(experts * 8 * WINDOW * padded * features * 2, 20e6),
        name="dispatch_gated" if gated else "dispatch",
    )(table, *shards, slots, *([gates] if gated else []))


def expert_kernel(layout, *refs):
    info_ref, x_ref, dy_ref = refs[:3]
    w_refs = refs[3:11]
    y_ref, dx_ref, keep_ref, send_ref = refs[11:15]
    w_in, w_out, g_in, g_out = refs[15:]
    place = info_ref[0]
    count = info_ref[1 + pl.program_id(0)]
    features = w_in.shape[0]
    block = features // OUTER
    for ref, flip in zip(w_refs, layout):
        row = pl.multiple_of((place ^ flip) * block, 16)
        w_in[pl.ds(row, block), :] = ref[0, 0]
        w_out[pl.ds(row, block), :] = ref[0, 1]
    g_in[...] = jnp.zeros_like(g_in)
    g_out[...] = jnp.zeros_like(g_out)
    tiles = (count + ROW_TILE - 1) // ROW_TILE

    def tile(i, carry):
        rows = pl.ds(pl.multiple_of(i * ROW_TILE, 16), ROW_TILE)
        x = x_ref[0, rows, :]
        dy = dy_ref[0, rows, :]
        pre = dot(x, w_in[...])
        share = 0.5 * (1.0 + lax.erf(pre * (1.0 / math.sqrt(2.0))))
        hid = (pre * share).astype(BF16)
        slope = share + pre * jnp.exp(-0.5 * pre * pre) * (1.0 / math.sqrt(2.0 * math.pi))
        y_ref[0, rows, :] = dot(hid, w_out[...], ((1,), (1,))).astype(BF16)
        dpre = (dot(dy, w_out[...]) * slope).astype(BF16)
        dx_ref[0, rows, :] = dot(dpre, w_in[...], ((1,), (1,))).astype(BF16)
        g_in[...] += dot(x, dpre, ((0,), (0,)))
        g_out[...] += dot(dy, hid, ((0,), (0,)))
        return carry

    lax.fori_loop(0, tiles, tile, 0)
    rest = pl.ds(pl.multiple_of(tiles * ROW_TILE, 16), WINDOW + 16)
    y_ref[0, rest, :] = jnp.zeros((WINDOW + 16, features), BF16)
    dx_ref[0, rest, :] = jnp.zeros((WINDOW + 16, features), BF16)
    for number in range(OUTER):
        flip = block_flip(number >> 2 & 1, number & 1, number >> 1 & 1)
        row = pl.multiple_of((place ^ flip) * block, 16)
        target = send_ref if number >= OUTER // 2 else keep_ref
        at = slice(number % (OUTER // 2) * block, (number % (OUTER // 2) + 1) * block)
        target[0, 0, at, :] = g_in[pl.ds(row, block), :].astype(BF16)
        target[0, 1, at, :] = g_out[pl.ds(row, block), :].astype(BF16)


def expert_math(info, x, dy, weights, layout, first, limit):
    experts = weights[0].shape[0]
    length, features = x.shape[1:]
    hidden = weights[0].shape[3]
    most = up(limit, ROW_TILE)
    slots_spec = pl.BlockSpec((1, most, features), lambda e: (e + first, 0, 0))
    out_spec = pl.BlockSpec((1, length, features), lambda e: (e, 0, 0))
    share = sds((experts, 2, features // 2, hidden), BF16)
    share_spec = pl.BlockSpec((1, 2, features // 2, hidden), lambda e: (e, 0, 0, 0))
    return pl.pallas_call(
        functools.partial(expert_kernel, layout),
        grid=(experts,),
        out_shape=(sds((experts, length, features), BF16),) * 2 + (share,) * 2,
        in_specs=[smem_spec(), slots_spec, slots_spec]
        + [pl.BlockSpec((1,) + w.shape[1:], lambda e: (e, 0, 0, 0)) for w in weights],
        out_specs=(out_spec, out_spec, share_spec, share_spec),
        scratch_shapes=[
            pltpu.VMEM((features, hidden), BF16),
            pltpu.VMEM((features, hidden), BF16),
            pltpu.VMEM((features, hidden), F32),
            pltpu.VMEM((features, hidden), F32),
        ],
        compiler_params=params(60),
        cost_estimate=cost(experts * 12 * limit * features * hidden, 30e6, 4e6),
        name="expert_math",
    )(info, x, dy, *weights)


def combine_kernel(gated, n_sources, *refs):
    table_ref = refs[0]
    source_refs = refs[1 : 1 + n_sources]
    slot_ref = refs[1 + n_sources]
    gate_ref = refs[2 + n_sources] if gated else None
    send_ref, keep_ref, window = refs[-3:]
    r = pl.program_id(0)
    n_shards = pl.num_programs(0)
    per_source = source_refs[0].shape[0]
    experts = per_source * n_sources
    shard = lax.rem(r + n_shards // 2, n_shards)
    padded = slot_ref.shape[1]
    lanes = lax.broadcasted_iota(jnp.int32, (padded, WINDOW), 1)

    def chosen(e, low):
        hit = slot_ref[0, :, e : e + 1] == lanes + low
        return jnp.where(hit, gate_ref[0, :, e : e + 1] if gated else 1.0, 0.0).astype(BF16)

    firsts, steps, parts = [], [], []
    for e in range(experts):
        start = table_ref[e * n_shards + shard]
        number = table_ref[n_shards * experts + e * n_shards + shard]
        first = pl.multiple_of(start // 16 * 16, 16)
        firsts.append(first)
        steps.append((start - first + number + WINDOW - 1) // WINDOW)
        window[e * WINDOW : (e + 1) * WINDOW, :] = source_refs[e // per_source][e % per_source, pl.ds(first, WINDOW), :]
        parts.append(chosen(e, first))
    total = dot(jnp.concatenate(parts, 1), window[...]).astype(BF16)

    def finish(ref):
        ref[0] = total
        for e in range(experts):

            def step(c, carry, e=e):
                low = pl.multiple_of(firsts[e] + c * WINDOW, 16)
                rows = source_refs[e // per_source][e % per_source, pl.ds(low, WINDOW), :]
                ref[0] = (ref[0].astype(F32) + dot(chosen(e, low), rows)).astype(BF16)
                return carry

            lax.fori_loop(1, steps[e], step, 0)

    @pl.when(r < n_shards // 2)
    def _():
        finish(send_ref)

    @pl.when(r >= n_shards // 2)
    def _():
        finish(keep_ref)


def combine(table, sources, slots, gates):
    n_shards, padded, experts = slots.shape
    features = sources[0].shape[2]
    gated = gates is not None
    half = n_shards // 2
    per_shard = pl.BlockSpec((1, padded, experts), lambda r: (lax.rem(r + half, n_shards), 0, 0))
    share = sds((half, padded, features), BF16)
    return pl.pallas_call(
        functools.partial(combine_kernel, gated, len(sources)),
        grid=(n_shards,),
        out_shape=(share, share),
        in_specs=[smem_spec()] + [vmem_spec()] * len(sources) + [per_shard] * (2 if gated else 1),
        out_specs=(
            pl.BlockSpec((1, padded, features), lambda r: (jnp.minimum(r, half - 1), 0, 0)),
            pl.BlockSpec((1, padded, features), lambda r: (jnp.maximum(r - half, 0), 0, 0)),
        ),
        scratch_shapes=[pltpu.VMEM((experts * WINDOW, features), BF16)],
        compiler_params=params(48),
        cost_estimate=cost(n_shards * experts * WINDOW * padded * features * 2, 20e6),
        name="combine_gated" if gated else "combine",
    )(table, *sources, slots, *([gates] if gated else []))


def spread_kernel(images, stride, x_ref, out_ref, scratch):
    spread_rows(x_ref, scratch, images, stride)
    out_ref[...] = scratch[...].astype(BF16)


def spread(rows, images, stride, padded):
    return pl.pallas_call(
        functools.partial(spread_kernel, images, stride),
        out_shape=sds((padded, rows.shape[1]), BF16),
        in_specs=[vmem_spec()],
        out_specs=vmem_spec(),
        scratch_shapes=[pltpu.VMEM((padded, rows.shape[1]), F32)],
        compiler_params=params(16),
        cost_estimate=cost(1e6, 3e6),
        name="spread_rows",
    )(rows)


def finish_kernel(images, stride, res_ref, a_ref, b_ref, c_ref, out_ref, scratch):
    mixture = a_ref[...].astype(F32) + b_ref[...].astype(F32) + c_ref[...].astype(F32)
    scratch[...] = res_ref[...] + mixture
    gather_rows(scratch, out_ref, images, stride)


def finish(residual, pieces, tokens, images, stride):
    return pl.pallas_call(
        functools.partial(finish_kernel, images, stride),
        out_shape=sds((tokens, residual.shape[1]), F32),
        in_specs=[vmem_spec()] * 4,
        out_specs=vmem_spec(),
        scratch_shapes=[pltpu.VMEM(residual.shape, F32)],
        compiler_params=params(24),
        cost_estimate=cost(1e6, 6e6),
        name="finish_rows",
    )(residual, *pieces)


def body(
    sizes,
    block_input,
    cotangent,
    query_weight,
    key_weight,
    value_weight,
    output_weight,
    first_gain,
    first_shift,
    expert_in,
    expert_out,
    second_gain,
    second_shift,
    routes,
    route_gates,
    clip_threshold,
):
    dp, tensor = sizes["dp"], sizes["tensor"]
    inner = dp // OUTER
    tokens, features = block_input.shape
    columns = query_weight.shape[1]
    heads = columns // HD
    images = tokens // SEQ
    stride = up(SEQ, 8)
    padded = up(images * stride, 16)
    experts = expert_in.shape[0]
    mine = experts // 2
    half = mine // 2
    block = features // OUTER
    limit = 2 * CAP
    dp_at = lax.axis_index("dp")
    place = dp_at // inner
    tensor_at = lax.axis_index("tensor")
    low_bit = place >> 1 & 1

    def along(axis, size, flip):
        pairs = [(i, i ^ flip) for i in range(size)]
        return lambda value: lax.ppermute(value, axis, pairs)

    send_x = along("dp", dp, 1 * inner)
    send_low = along("dp", dp, 2 * inner)
    send_high = along("dp", dp, 4 * inner)
    send_core = along("tensor", tensor, 1)
    send_y = along("tensor", tensor, 2)

    def whole_block(value, axis):
        if inner == 1:
            return value
        every = lax.all_gather(value, "dp", axis=axis, tiled=True)
        return lax.dynamic_slice_in_dim(every, place * block, block, axis)

    def own_rows(value, axis):
        if inner == 1:
            return value
        shape = list(value.shape)
        shape[axis] = features
        every = lax.dynamic_update_slice_in_dim(jnp.zeros(shape, value.dtype), value, place * block, axis)
        return lax.psum_scatter(every, "dp", scatter_dimension=axis, tiled=True)

    packed = jnp.concatenate(
        (output_weight.T, query_weight, key_weight, value_weight), 1
    ).astype(BF16)
    packed = whole_block(packed, 0)
    norms = jnp.stack((first_gain, first_shift, second_gain, second_shift)).astype(BF16)
    norms = whole_block(norms, 1)
    norms = lax.dynamic_update_slice(jnp.zeros((EXTRA, features), BF16), norms, (0, place * block))
    own = jnp.concatenate((packed, norms), 0)[None]
    pair = jnp.concatenate((own, send_high(own)), 0)
    four = jnp.concatenate((pair, send_low(pair)), 0)
    four_x = send_x(four)
    four_y = send_y(four)
    two_a = send_x(four_y[:2])
    two_b = send_y(four_x[2:])

    def entries(t, x_bit, lows=(0, 1)):
        return tuple((t, block_flip(x_bit, low, high)) for low in lows for high in (0, 1))

    pieces = [four, four_x, four_y, two_a, two_b]
    layout = [entries(0, 0), entries(0, 1), entries(1, 0), entries(1, 1, (0,)), entries(1, 1, (1,))]
    for piece in (four, four_x, four_y, two_a, two_b):
        pieces.append(send_core(piece))
    layout += [tuple((t + 2, flip) for t, flip in group) for group in layout[:5]]
    gains = jnp.sum(jnp.concatenate((four[:, block:], four_x[:, block:]), 0).astype(F32), 0)

    w_in = whole_block(expert_in.astype(BF16), 1)
    w_out = whole_block(expert_out.astype(BF16), 2).swapaxes(1, 2)
    both = jnp.stack((w_in, w_out), 1)
    both, _ = lax.optimization_barrier((both, four))
    chunks = []
    for c in range(2):
        keep = lax.dynamic_slice_in_dim(both, low_bit * mine + c * half, half, 0)
        give = lax.dynamic_slice_in_dim(both, (1 - low_bit) * mine + c * half, half, 0)
        got_low = send_low(give)
        got = [keep, got_low, send_high(keep), send_high(got_low)]
        got += [send_x(w) for w in got]
        chunks.append(got)
    expert_layout = tuple(
        block_flip(x_bit, low, high) for x_bit in (0, 1) for high in (0, 1) for low in (0, 1)
    )

    table = jnp.concatenate((routes.T.astype(F32), route_gates.T), 0)
    picks = routes.shape[1]
    table = table.reshape(2 * picks, tensor, images, SEQ)
    table = jnp.pad(table, ((0, 0), (0, 0), (0, 0), (0, stride - SEQ)), constant_values=-1)
    table = table.reshape(2 * picks, tensor, images * stride)
    table = jnp.pad(table, ((0, 0), (0, 0), (0, padded - images * stride)), constant_values=-1)
    table = jnp.stack((table, send_low(table)))
    table = table.reshape(2, 2 * picks, 2, 2, padded)
    table = jnp.where(tensor_at >> 1 & 1 == 1, table[:, :, ::-1], table)
    table = jnp.where(tensor_at & 1 == 1, table[:, :, :, ::-1], table)
    table = table.transpose(1, 3, 0, 2, 4).reshape(2 * picks, 8, padded)
    ids = (low_bit * mine + jnp.arange(mine)).astype(F32)[None, :, None, None]
    hits = table[:picks, None] == ids
    chosen = jnp.any(hits, 0)
    gates = jnp.sum(jnp.where(hits, table[picks:, None], 0.0), 0)
    order = lax.broadcasted_iota(jnp.int32, (padded, padded), 0) < lax.broadcasted_iota(
        jnp.int32, (padded, padded), 1
    )
    before = jnp.dot(
        chosen.reshape(-1, padded).astype(BF16), order.astype(BF16), preferred_element_type=F32
    ).reshape(chosen.shape)
    counts = jnp.sum(chosen.astype(F32), -1)
    ahead = (jnp.arange(8)[:, None] < jnp.arange(8)[None, :]).astype(F32)
    starts = jnp.sum(counts[:, :, None] * ahead[None], 1)
    slots = jnp.where(chosen, starts[:, :, None] + before, -1.0).astype(jnp.int32)
    totals = jnp.sum(counts, 1)
    scalars = jnp.concatenate((starts.reshape(-1), counts.reshape(-1), totals)).astype(jnp.int32)
    slot_columns = slots.transpose(1, 2, 0)
    gate_columns = gates.transpose(1, 2, 0)

    def everyone(rows):
        by_low = send_low(rows)
        by_y = send_y(rows)
        near = [rows, by_y, by_low, send_y(by_low)]
        return near + [send_core(piece) for piece in near]

    def to_owner(send, keep):
        near = send_core(send)
        sums = [keep[i] + near[i] for i in range(4)]
        far = sums[2] + send_y(sums[3])
        return (sums[0], send_y(sums[1]), send_low(far))

    cot_half = spread(cotangent, images, stride, padded)
    cot_slots = dispatch(scalars, everyone(cot_half), slots, gates, limit)

    place_word = place.astype(jnp.int32).reshape(1)
    residual, second, first, weights, kept, peaks = attention_forward(
        place_word, block_input, gains, pieces, layout, images, stride, padded, tensor, heads
    )

    x_slots = dispatch(scalars, everyone(second), slots, None, limit)
    results, shares = [], []
    for c in range(2):
        info = jnp.concatenate((place_word, totals[c * half : (c + 1) * half].astype(jnp.int32)))
        y, dx, keep, send = expert_math(
            info, x_slots, cot_slots, chunks[c], expert_layout, c * half, limit
        )
        results.append((y, dx))
        rows = keep.shape[2] // 2
        other = send_x(send)
        far = send_high(keep[:, :, rows:] + other[:, :, rows:])
        near = (keep[:, :, :rows] + other[:, :, :rows]).astype(F32) + far.astype(F32)
        shares.append((near[:, :, :block], send_low(near[:, :, block:].astype(BF16))))
    grad_pieces = to_owner(*combine(scalars, [dx for _, dx in results], slot_columns, None))
    mixture_pieces = to_owner(*combine(scalars, [y for y, _ in results], slot_columns, gate_columns))

    peak = peaks[:, 0, :heads].reshape(2, 2, heads)
    peak = jnp.where(tensor_at & 1 == 1, peak[::-1], peak)
    peak = jnp.where(tensor_at >> 1 & 1 == 1, peak[:, ::-1], peak)
    peak = peak.transpose(1, 0, 2).reshape(tensor * heads)
    extra = jnp.zeros((EXTRA, features), F32)
    if inner == 1:
        device = dp_at * tensor + tensor_at
        high = lax.reduce_precision(peak, 8, 7)
        rest = lax.reduce_precision(peak - high, 8, 7)
        is_mine = (jnp.arange(dp * tensor) == device)[None, :, None]
        words = jnp.where(is_mine, jnp.stack((high, rest))[:, None, :], 0.0).reshape(2, -1)
        extra = extra.at[4:6, : words.shape[1]].set(words)
    input_grad, keep, send = attention_backward(
        block_input, cotangent, residual, grad_pieces, first, weights, kept, gains, extra, images, stride, heads
    )
    block_output = finish(residual, mixture_pieces, tokens, images, stride)

    own_share = jnp.concatenate([near for near, _ in shares], 0).astype(BF16)
    far_share = jnp.concatenate([far for _, far in shares], 0)
    grads = jnp.concatenate(
        (
            jnp.where(low_bit == 0, own_share, far_share),
            jnp.where(low_bit == 0, far_share, own_share),
        ),
        0,
    ).astype(F32)
    expert_in_grad = own_rows(grads[:, 0], 1)
    expert_out_grad = own_rows(grads[:, 1].swapaxes(1, 2), 2)

    near = send_core(send)
    upper = send_y(keep[1] + near[1])
    total = keep[0] + near[0] + upper
    if inner == 1:
        total = lax.all_to_all(total, "dp", 0, 0, tiled=True)
        total = jnp.sum(total.astype(F32), 0)
        words = total[block:]
        total = total[:block]
        peak = jnp.sum(words[4:6, : dp * tensor * tensor * heads], 0).reshape(dp * tensor, tensor * heads)
        peak = jnp.max(peak, 0)
    else:
        words = lax.psum(total[0, block:].astype(F32), "dp")
        total = total[:, :block].reshape(features, features).astype(F32)
        total = lax.psum_scatter(total, "dp", scatter_dimension=0, tiled=True)
        peak = lax.pmax(peak, ("dp", "tensor"))
    head_maxima = lax.dynamic_slice_in_dim(peak, tensor_at * heads, heads, 0)
    vectors = lax.dynamic_slice_in_dim(words[:4], dp_at * (features // dp), features // dp, 1)
    output_grad, query_grad, key_grad, value_grad = (
        total[:, i * columns : (i + 1) * columns] for i in range(4)
    )
    factor = jnp.minimum(1.0, clip_threshold / jnp.maximum(head_maxima, 1.0))
    column_scale = jnp.repeat(jnp.sqrt(factor), HD)
    return (
        block_output,
        input_grad,
        query_grad,
        key_grad,
        value_grad,
        output_grad.T,
        vectors[0],
        vectors[1],
        expert_in_grad,
        expert_out_grad,
        vectors[2],
        vectors[3],
        query_weight * column_scale[None, :],
        key_weight * column_scale[None, :],
        head_maxima,
    )


def solution(mesh):
    rows = P(("dp", "tensor"), None)
    by_column, by_row, by_dp = P("dp", "tensor"), P("tensor", "dp"), P("dp")
    up_spec, down_spec = P(None, "dp", "tensor"), P(None, "tensor", "dp")
    sizes = dict(mesh.shape)
    return jax.shard_map(
        functools.partial(body, sizes),
        mesh=mesh,
        in_specs=(
            rows, rows, by_column, by_column, by_column, by_row, by_dp, by_dp, up_spec, down_spec,
            by_dp, by_dp, P("dp", None), P("dp", None), P("tensor"),
        ),
        out_specs=(
            rows, rows, by_column, by_column, by_column, by_row, by_dp, by_dp, up_spec, down_spec,
            by_dp, by_dp, by_column, by_column, P("tensor"),
        ),
        check_vma=False,
    )
```

```python
import functools
import math

import jax
import jax.numpy as jnp
from jax import lax
from jax.experimental import pallas as pl
from jax.experimental.pallas import tpu as pltpu
from jax.sharding import PartitionSpec as P

HD = 64
SEQ = 197
CAP = 792
EPSILON = 1e-06
F32 = jnp.float32
BF16 = jnp.bfloat16
OUTER = 8
EXTRA = 16
ROW_TILE = 256
WINDOW = 256
MIB = 1 << 20


def up(number, unit):
    return -(-number // unit) * unit


def dot(left, right, contract=((1,), (0,))):
    return lax.dot_general(left, right, (contract, ((), ())), preferred_element_type=F32)


def params(mib):
    return pltpu.CompilerParams(vmem_limit_bytes=mib * MIB)


def any_spec():
    return pl.BlockSpec(memory_space=pl.ANY)


def vmem_spec():
    return pl.BlockSpec(memory_space=pltpu.VMEM)


def smem_spec():
    return pl.BlockSpec(memory_space=pltpu.SMEM)


def sds(shape, dtype):
    return jax.ShapeDtypeStruct(shape, dtype)


def cost(microseconds):
    return pl.CostEstimate(flops=int(microseconds * 0.5e9), bytes_accessed=0, transcendentals=0)


def after(value, *others):
    return lax.optimization_barrier((value, *others))[0]


def block_flip(x_bit, low_bit, high_bit):
    return x_bit | low_bit << 1 | high_bit << 2


def norm_stats(values):
    mean = jnp.mean(values, -1, keepdims=True)
    centred = values - mean
    scale = lax.rsqrt(jnp.mean(centred * centred, -1, keepdims=True) + EPSILON)
    return centred * scale, scale


def spread_rows(source, target, images, stride):
    for i in range(images):
        target[i * stride : i * stride + SEQ, :] = source[i * SEQ : (i + 1) * SEQ, :].astype(F32)
        end = (i + 1) * stride if i + 1 < images else target.shape[0]
        target[i * stride + SEQ : end, :] = jnp.zeros((end - i * stride - SEQ, target.shape[1]), F32)


def gather_rows(source, target, images, stride):
    for i in range(images):
        target[i * SEQ : (i + 1) * SEQ, :] = source[i * stride : i * stride + SEQ, :]


def attention_forward_kernel(images, stride, heads, layout, *refs):
    n_pieces = len(layout)
    place_ref, x_ref, gains_ref = refs[:3]
    piece_refs = refs[3 : 3 + n_pieces]
    res_ref, second_ref, first_ref, w_ref, kept_ref, peak_ref = refs[3 + n_pieces : 9 + n_pieces]
    scratch, sems = refs[9 + n_pieces :]
    columns = heads * HD
    block = w_ref.shape[1] // OUTER
    place = place_ref[0]
    copies = []
    for ref, entries in zip(piece_refs, layout):
        for j, (t, flip) in enumerate(entries):
            row = pl.multiple_of((place ^ flip) * block, 16)
            copies.append(
                pltpu.make_async_copy(
                    ref.at[j, pl.ds(0, block), :],
                    w_ref.at[t, pl.ds(row, block), :],
                    sems.at[len(copies)],
                )
            )
            copies[-1].start()
    spread_rows(x_ref, res_ref, images, stride)
    unit, _ = norm_stats(res_ref[...])
    first_ref[...] = (unit * gains_ref[0:1, :] + gains_ref[1:2, :]).astype(BF16)
    for copy in copies:
        copy.wait()
    scale = 1.0 / math.sqrt(HD)
    key_ok = lax.broadcasted_iota(jnp.int32, (stride, stride), 0) < SEQ
    query_ok = lax.broadcasted_iota(jnp.int32, (1, stride), 1) < SEQ
    lane = lax.broadcasted_iota(jnp.int32, (8, 128), 1)

    def step(t, carry):
        scratch[...] = dot(first_ref[...], w_ref[t]).astype(BF16).astype(F32)
        peaks = jnp.full((8, 128), -jnp.inf, F32)
        for i in range(images):
            rows = slice(i * stride, (i + 1) * stride)
            for h in range(heads):
                at = [slice((1 + p) * columns + h * HD, (1 + p) * columns + (h + 1) * HD) for p in range(3)]
                q = (scratch[rows, at[0]] * scale).astype(BF16)
                k = scratch[rows, at[1]].astype(BF16)
                v = scratch[rows, at[2]].astype(BF16)
                s = jnp.where(key_ok, dot(k, q, ((1,), (1,))), -1e30)
                top = jnp.max(s, 0, keepdims=True)
                e = jnp.exp(s - top)
                p = e * (1.0 / jnp.sum(e, 0, keepdims=True))
                o = dot(v, p.astype(BF16), ((0,), (0,))).T
                scratch[rows, h * HD : (h + 1) * HD] = o.astype(BF16).astype(F32)
                peak = jnp.max(jnp.where(query_ok, top, -jnp.inf), keepdims=True)
                peaks = jnp.maximum(peaks, jnp.where(lane == h, peak, -jnp.inf))
        peak_ref[t] = peaks
        kept_ref[t] = scratch[...].astype(BF16)
        res_ref[...] += dot(kept_ref[t, :, 0:columns], w_ref[t, :, 0:columns], ((1,), (1,)))
        return carry

    lax.fori_loop(0, w_ref.shape[0], step, 0)
    unit, _ = norm_stats(res_ref[...])
    second_ref[...] = (unit * gains_ref[2:3, :] + gains_ref[3:4, :]).astype(BF16)


def attention_forward(place, rows, gains, pieces, layout, images, stride, padded, parts, heads):
    features = rows.shape[1]
    n_copies = sum(len(entries) for entries in layout)
    return pl.pallas_call(
        functools.partial(attention_forward_kernel, images, stride, heads, layout),
        out_shape=(
            sds((padded, features), F32),
            sds((padded, features), BF16),
            sds((padded, features), BF16),
            sds((parts, features, features), BF16),
            sds((parts, padded, features), BF16),
            sds((parts, 8, 128), F32),
        ),
        in_specs=[smem_spec(), vmem_spec(), vmem_spec()] + [any_spec()] * len(pieces),
        out_specs=(vmem_spec(),) * 6,
        scratch_shapes=[
            pltpu.VMEM((padded, features), F32),
            pltpu.SemaphoreType.DMA((n_copies,)),
        ],
        compiler_params=params(48),
        cost_estimate=cost(22),
        name="attention_forward",
    )(place, rows, gains, *pieces)


def head_at(columns, part, head):
    return slice(part * columns + head * HD, part * columns + (head + 1) * HD)


def norm_back(grad, gain, unit, scale):
    weighted = grad * gain
    mean = jnp.mean(weighted, -1, keepdims=True)
    return (weighted - mean - unit * jnp.mean(weighted * unit, -1, keepdims=True)) * scale


def heads_backward(images, stride, heads, t, w_ref, kept_ref, half_ref, firsts, halves, kept, mixed, grads, total):
    columns = heads * HD
    features = w_ref.shape[2]
    scale = 1.0 / math.sqrt(HD)
    key_ok = lax.broadcasted_iota(jnp.int32, (stride, stride), 0) < SEQ
    kept[...] = kept_ref[t, 0].astype(F32)
    mixed[...] = dot(half_ref[...], w_ref[t, 0, :, 0:columns]).astype(BF16).astype(F32)
    for i in range(images):
        rows = slice(i * stride, (i + 1) * stride)
        for h in range(heads):
            q = (kept[rows, head_at(columns, 1, h)] * scale).astype(BF16)
            k = kept[rows, head_at(columns, 2, h)].astype(BF16)
            v = kept[rows, head_at(columns, 3, h)].astype(BF16)
            do = mixed[rows, h * HD : (h + 1) * HD].astype(BF16)
            s = jnp.where(key_ok, dot(k, q, ((1,), (1,))), -1e30)
            e = jnp.exp(s - jnp.max(s, 0, keepdims=True))
            p = e * (1.0 / jnp.sum(e, 0, keepdims=True))
            dp = dot(v, do, ((1,), (1,)))
            dv = dot(p.astype(BF16), do)
            ds = (p * (dp - jnp.sum(p * dp, 0, keepdims=True))).astype(BF16)
            dq = dot(k, ds, ((0,), (0,))).T * scale
            dk = dot(ds, q)
            grads[rows, head_at(columns, 1, h)] = dq
            grads[rows, head_at(columns, 2, h)] = dk
            grads[rows, head_at(columns, 3, h)] = dv
    packed = grads[...].astype(BF16)
    total[...] += dot(packed, w_ref[t, 0], ((1,), (1,)))
    full = dot(firsts[...], packed)
    out = dot(halves[...], kept_ref[t, 0, :, 0:columns])
    full = full + jnp.concatenate((out, jnp.zeros((features, features - columns), F32)), 1)
    return full.astype(BF16)


def half_spec(value, y):
    return pl.BlockSpec((2, 1) + value.shape[2:], lambda i: (0, y, 0, 0))


def put_blocks(refs, t, full):
    block = full.shape[0] // OUTER
    for i, ref in enumerate(refs):

        @pl.when(t == i)
        def _(ref=ref):
            for j in range(OUTER):
                ref[j, 0:block, :] = full[j * block : (j + 1) * block, :]


def attention_backward_kernel(images, stride, heads, *refs):
    (cot_ref, res_ref, d0_ref, d1_ref, d2_ref, first_ref, w_ref, kept_ref, gains_ref, extra_ref) = refs[:10]
    keep_ref, send_ref, resid, half, total, firsts, halves, more_ref = refs[10:18]
    kept, grads, mixed = refs[18:]
    features = w_ref.shape[2]
    unit, scale_two = norm_stats(res_ref[...])
    da2 = d0_ref[...].astype(F32) + d1_ref[...].astype(F32) + d2_ref[...].astype(F32)
    row = lax.broadcasted_iota(jnp.int32, (EXTRA, features), 0)
    extra = jnp.where(row == 2, jnp.sum(da2 * unit, 0, keepdims=True), extra_ref[...])
    more_ref[...] = jnp.where(row == 3, jnp.sum(da2, 0, keepdims=True), extra)
    spread_rows(cot_ref, resid, images, stride)
    resid[...] += norm_back(da2, gains_ref[2:3, :], unit, scale_two)
    half[...] = resid[...].astype(BF16)
    firsts[...] = first_ref[...].T
    halves[...] = half[...].T
    total[...] = jnp.zeros_like(total)
    grads[...] = jnp.zeros_like(grads)

    def step(t, carry):
        full = heads_backward(
            images, stride, heads, t, w_ref, kept_ref, half, firsts, halves, kept, mixed, grads, total
        )
        put_blocks((keep_ref, send_ref), t, full)
        return carry

    lax.fori_loop(0, 2, step, 0)


def attention_rest_kernel(images, stride, heads, *refs):
    (x_ref, resid_ref, half, total_ref, firsts, halves, w_ref, kept_ref, gains_ref, more_ref) = refs[:10]
    input_grad_ref, keep_ref, send_ref, extra_ref = refs[10:14]
    kept, grads, mixed, total = refs[14:]
    features = w_ref.shape[2]
    block = features // OUTER
    total[...] = total_ref[...]
    grads[...] = jnp.zeros_like(grads)

    def step(t, carry):
        full = heads_backward(
            images, stride, heads, t, w_ref, kept_ref, half, firsts, halves, kept, mixed, grads, total
        )
        put_blocks((keep_ref, send_ref), t, full)
        return carry

    lax.fori_loop(0, 2, step, 0)
    spread_rows(x_ref, kept, images, stride)
    unit, scale_one = norm_stats(kept[...])
    da = total[...]
    grads[...] = resid_ref[...] + norm_back(da, gains_ref[0:1, :], unit, scale_one)
    gather_rows(grads, input_grad_ref, images, stride)
    row = lax.broadcasted_iota(jnp.int32, (EXTRA, features), 0)
    extra = jnp.where(row == 0, jnp.sum(da * unit, 0, keepdims=True), more_ref[...])
    extra = jnp.where(row == 1, jnp.sum(da, 0, keepdims=True), extra).astype(BF16)
    extra_ref[...] = extra
    for ref in (keep_ref, send_ref):
        for j in range(OUTER):
            ref[j, block : block + EXTRA, :] = extra


def attention_backward(cot, residual, pieces, first, weights, kept, gains, extra, images, stride, heads):
    padded, features = first.shape
    share = sds((OUTER, features // OUTER, features), BF16)
    wide, half, turned = sds((padded, features), F32), sds((padded, features), BF16), sds((features, padded), BF16)
    return pl.pallas_call(
        functools.partial(attention_backward_kernel, images, stride, heads),
        grid=(1,),
        out_shape=(share, share, wide, half, wide, turned, turned, sds((EXTRA, features), F32)),
        in_specs=[vmem_spec()] * 6 + [half_spec(weights, 1), half_spec(kept, 1)] + [vmem_spec()] * 2,
        out_specs=(vmem_spec(),) * 8,
        scratch_shapes=[
            pltpu.VMEM((padded, features), F32),
            pltpu.VMEM((padded, features), F32),
            pltpu.VMEM((padded, heads * HD), F32),
        ],
        compiler_params=params(50),
        cost_estimate=cost(20),
        name="attention_backward",
    )(cot, residual, *pieces, first, weights, kept, gains, extra)


def attention_rest(rows, resid, half, total, firsts, halves, weights, kept, gains, more, images, stride, heads):
    padded, features = resid.shape
    share = sds((OUTER, features // OUTER + EXTRA, features), BF16)
    return pl.pallas_call(
        functools.partial(attention_rest_kernel, images, stride, heads),
        grid=(1,),
        out_shape=(sds(rows.shape, F32), share, share, sds((EXTRA, features), BF16)),
        in_specs=[vmem_spec()] * 6 + [half_spec(weights, 0), half_spec(kept, 0)] + [vmem_spec()] * 2,
        out_specs=(vmem_spec(),) * 4,
        scratch_shapes=[
            pltpu.VMEM((padded, features), F32),
            pltpu.VMEM((padded, features), F32),
            pltpu.VMEM((padded, heads * HD), F32),
            pltpu.VMEM((padded, features), F32),
        ],
        compiler_params=params(50),
        cost_estimate=cost(20),
        name="attention_backward_rest",
    )(rows, resid, half, total, firsts, halves, weights, kept, gains, more)


def dispatch_kernel(gated, *refs):
    table_ref = refs[0]
    slot_ref = refs[-3] if gated else refs[-2]
    gate_ref = refs[-2] if gated else None
    out_ref = refs[-1]
    shard_refs = []
    for ref in refs[1 : -3 if gated else -2]:
        shard_refs += [ref] if len(ref.shape) == 2 else [ref.at[i] for i in range(ref.shape[0])]
    n_shards = len(shard_refs)
    expert = pl.program_id(0)
    experts = pl.num_programs(0)
    padded = shard_refs[0].shape[0]
    features = shard_refs[0].shape[1]
    count_all = table_ref[2 * n_shards * experts + expert]
    tail = pl.multiple_of(count_all // 16 * 16, 16)
    out_ref[0, pl.ds(tail, ROW_TILE + 16), :] = jnp.zeros((ROW_TILE + 16, features), BF16)
    row16 = lax.broadcasted_iota(jnp.int32, (16, 1), 0)
    rows = lax.broadcasted_iota(jnp.int32, (WINDOW, padded), 0)
    starts = [table_ref[expert * n_shards + r] for r in range(n_shards)]
    numbers = [table_ref[n_shards * experts + expert * n_shards + r] for r in range(n_shards)]
    firsts = [start // 16 * 16 for start in starts]
    steps = [
        (start - first + number + WINDOW - 1) // WINDOW
        for start, first, number in zip(starts, firsts, numbers)
    ]

    def step(r, c):
        low = pl.multiple_of(firsts[r] + c * WINDOW, 16)
        hit = slot_ref[0, r : r + 1, :] - low == rows
        chosen = jnp.where(hit, 1.0, 0.0)
        got = dot(chosen.astype(BF16), shard_refs[r][...])
        if gated:
            got = got * jnp.sum(chosen * gate_ref[0, r : r + 1, :], -1, keepdims=True)
        got = got.astype(BF16)
        before = out_ref[0, pl.ds(low, 16), :]
        out_ref[0, pl.ds(low, 16), :] = jnp.where(row16 + low < starts[r], before, got[:16])
        out_ref[0, pl.ds(low + 16, WINDOW - 16), :] = got[16:]

    short = functools.reduce(jnp.maximum, steps) <= 1

    @pl.when(short)
    def _():
        for r in range(n_shards):
            step(r, 0)

    @pl.when(jnp.logical_not(short))
    def _():
        for r in range(n_shards):

            def again(c, carry, r=r):
                step(r, c)
                return carry

            lax.fori_loop(0, steps[r], again, 0)


def slot_rows(limit):
    return up(limit, ROW_TILE) + WINDOW + 16


def dispatch(table, shards, slots, gates, limit):
    experts = slots.shape[0]
    padded, features = shards[0].shape[-2:]
    length = slot_rows(limit)
    gated = gates is not None
    per_expert = pl.BlockSpec((1,) + slots.shape[1:], lambda e: (e, 0, 0))
    return pl.pallas_call(
        functools.partial(dispatch_kernel, gated),
        grid=(experts,),
        out_shape=sds((experts, length, features), BF16),
        in_specs=[smem_spec()] + [vmem_spec()] * len(shards) + [per_expert] * (2 if gated else 1),
        out_specs=pl.BlockSpec((1, length, features), lambda e: (e, 0, 0)),
        compiler_params=params(48),
        cost_estimate=cost(15),
        name="dispatch_gated" if gated else "dispatch",
    )(table, *shards, slots, *([gates] if gated else []))


def normal_share(u):
    bell = jnp.exp(-0.5 * u * u)
    t = 1.0 / (1.0 + jnp.abs(u) * (0.3275911 / math.sqrt(2.0)))
    poly = 0.5 * 1.061405429
    for term in (-1.453152027, 1.421413741, -0.284496736, 0.254829592):
        poly = poly * t + 0.5 * term
    tail = poly * t * bell
    return jnp.where(u < 0, tail, 1.0 - tail), bell


def expert_kernel(*refs):
    info_ref, x_ref, dy_ref = refs[:3]
    w_refs = refs[3:11]
    y_ref, dx_ref = refs[11:13]
    share_refs = (refs[13:15], refs[15:17])
    w_in, w_out, g_in, g_out, hidden, slopes = refs[17:]
    place = info_ref[0]
    count = info_ref[1 + pl.program_id(0)]
    features = w_in.shape[0]
    block = features // OUTER
    for number, ref in enumerate(w_refs):
        flip = block_flip(number >> 2, number & 1, number >> 1 & 1)
        row = pl.multiple_of((place ^ flip) * block, 16)
        w_in[pl.ds(row, block), :] = ref[0, 0]
        w_out[pl.ds(row, block), :] = ref[0, 1]
    g_in[...] = jnp.zeros_like(g_in)
    g_out[...] = jnp.zeros_like(g_out)
    tiles = jnp.maximum((count + ROW_TILE - 1) // ROW_TILE, 1)

    def at(i):
        return pl.ds(pl.multiple_of(i * ROW_TILE, ROW_TILE), ROW_TILE)

    def first_half(i):
        pre = dot(x_ref[0, at(i), :], w_in[...])
        dh = dot(dy_ref[0, at(i), :], w_out[...])
        share, bell = normal_share(pre)
        hidden[i % 2] = (pre * share).astype(BF16)
        slope = share + pre * bell * (1.0 / math.sqrt(2.0 * math.pi))
        slopes[i % 2] = (dh * slope).astype(BF16)

    def second_half(i):
        hid, dpre = hidden[i % 2], slopes[i % 2]
        y_ref[0, at(i), :] = dot(hid, w_out[...], ((1,), (1,))).astype(BF16)
        dx_ref[0, at(i), :] = dot(dpre, w_in[...], ((1,), (1,))).astype(BF16)
        g_in[...] += dot(x_ref[0, at(i), :], dpre, ((0,), (0,)))
        g_out[...] += dot(dy_ref[0, at(i), :], hid, ((0,), (0,)))

    def tile(i, carry):
        second_half(i - 1)
        first_half(i)
        return carry

    first_half(0)
    lax.fori_loop(1, tiles, tile, 0)
    second_half(tiles - 1)
    rest = pl.ds(pl.multiple_of(tiles * ROW_TILE, 16), WINDOW + 16)
    y_ref[0, rest, :] = jnp.zeros((WINDOW + 16, features), BF16)
    dx_ref[0, rest, :] = jnp.zeros((WINDOW + 16, features), BF16)
    for number in range(OUTER):
        flip = block_flip(number >> 2 & 1, number & 1, number >> 1 & 1)
        row = pl.multiple_of((place ^ flip) * block, 16)
        in_ref, out_ref = share_refs[number // (OUTER // 2)]
        at = slice(number % (OUTER // 2) * block, (number % (OUTER // 2) + 1) * block)
        in_ref[0, at, :] = g_in[pl.ds(row, block), :].astype(BF16)
        out_ref[0, at, :] = g_out[pl.ds(row, block), :].astype(BF16)


def expert_math(info, x, dy, weights, first, experts, limit):
    length, features = x.shape[1:]
    hidden = weights[0].shape[3]
    most = up(limit, ROW_TILE)
    slots_spec = pl.BlockSpec((1, most, features), lambda e: (e + first, 0, 0))
    out_spec = pl.BlockSpec((1, length, features), lambda e: (e, 0, 0))
    share = sds((experts, features // 2, hidden), BF16)
    share_spec = pl.BlockSpec((1, features // 2, hidden), lambda e: (e, 0, 0))
    return pl.pallas_call(
        expert_kernel,
        grid=(experts,),
        out_shape=(sds((experts, length, features), BF16),) * 2 + (share,) * 4,
        in_specs=[smem_spec(), slots_spec, slots_spec]
        + [pl.BlockSpec((1,) + w.shape[1:], lambda e, at=first * (w.shape[0] > experts): (e + at, 0, 0, 0))
            for w in weights
],
        out_specs=(out_spec, out_spec) + (share_spec,) * 4,
        scratch_shapes=[
            pltpu.VMEM((features, hidden), BF16),
            pltpu.VMEM((features, hidden), BF16),
            pltpu.VMEM((features, hidden), F32),
            pltpu.VMEM((features, hidden), F32),
            pltpu.VMEM((2, ROW_TILE, hidden), BF16),
            pltpu.VMEM((2, ROW_TILE, hidden), BF16),
        ],
        compiler_params=params(60),
        cost_estimate=cost(33),
        name="expert_math",
    )(info, x, dy, *weights)


def combine_kernel(gated, n_sources, *refs):
    table_ref = refs[0]
    source_refs = refs[1 : 1 + n_sources]
    slot_ref = refs[1 + n_sources]
    gate_ref = refs[2 + n_sources] if gated else None
    send_ref, keep_ref, window = refs[-3:]
    r = pl.program_id(0)
    n_shards = pl.num_programs(0)
    per_source = source_refs[0].shape[0]
    experts = per_source * n_sources
    shard = lax.rem(r + n_shards // 2, n_shards)
    padded = slot_ref.shape[1]
    lanes = lax.broadcasted_iota(jnp.int32, (padded, WINDOW), 1)

    def chosen(e, low):
        hit = slot_ref[0, :, e : e + 1] == lanes + low
        return jnp.where(hit, gate_ref[0, :, e : e + 1] if gated else 1.0, 0.0).astype(BF16)

    firsts, steps, parts = [], [], []
    for e in range(experts):
        start = table_ref[e * n_shards + shard]
        number = table_ref[n_shards * experts + e * n_shards + shard]
        first = pl.multiple_of(start // 16 * 16, 16)
        firsts.append(first)
        steps.append((start - first + number + WINDOW - 1) // WINDOW)
        window[e * WINDOW : (e + 1) * WINDOW, :] = source_refs[e // per_source][e % per_source, pl.ds(first, WINDOW), :]
        parts.append(chosen(e, first))
    total = dot(jnp.concatenate(parts, 1), window[...]).astype(BF16)

    def finish(ref):
        ref[0] = total
        for e in range(experts):

            def step(c, carry, e=e):
                low = pl.multiple_of(firsts[e] + c * WINDOW, 16)
                rows = source_refs[e // per_source][e % per_source, pl.ds(low, WINDOW), :]
                ref[0] = (ref[0].astype(F32) + dot(chosen(e, low), rows)).astype(BF16)
                return carry

            lax.fori_loop(1, steps[e], step, 0)

    @pl.when(r < n_shards // 2)
    def _():
        finish(send_ref)

    @pl.when(r >= n_shards // 2)
    def _():
        finish(keep_ref)


def combine(table, sources, slots, gates):
    n_shards, padded, experts = slots.shape
    features = sources[0].shape[2]
    gated = gates is not None
    half = n_shards // 2
    per_shard = pl.BlockSpec((1, padded, experts), lambda r: (lax.rem(r + half, n_shards), 0, 0))
    share = sds((half, padded, features), BF16)
    return pl.pallas_call(
        functools.partial(combine_kernel, gated, len(sources)),
        grid=(n_shards,),
        out_shape=(share, share),
        in_specs=[smem_spec()] + [vmem_spec()] * len(sources) + [per_shard] * (2 if gated else 1),
        out_specs=(
            pl.BlockSpec((1, padded, features), lambda r: (jnp.minimum(r, half - 1), 0, 0)),
            pl.BlockSpec((1, padded, features), lambda r: (jnp.maximum(r - half, 0), 0, 0)),
        ),
        scratch_shapes=[pltpu.VMEM((experts * WINDOW, features), BF16)],
        compiler_params=params(48),
        cost_estimate=cost(2),
        name="combine_gated" if gated else "combine",
    )(table, *sources, slots, *([gates] if gated else []))


def spread_kernel(images, stride, x_ref, out_ref, scratch):
    spread_rows(x_ref, scratch, images, stride)
    out_ref[...] = scratch[...].astype(BF16)


def spread(rows, images, stride, padded):
    return pl.pallas_call(
        functools.partial(spread_kernel, images, stride),
        out_shape=sds((padded, rows.shape[1]), BF16),
        in_specs=[vmem_spec()],
        out_specs=vmem_spec(),
        scratch_shapes=[pltpu.VMEM((padded, rows.shape[1]), F32)],
        compiler_params=params(16),
        cost_estimate=cost(2),
        name="spread_rows",
    )(rows)


def finish_kernel(images, stride, res_ref, a_ref, b_ref, c_ref, out_ref, scratch):
    mixture = a_ref[...].astype(F32) + b_ref[...].astype(F32) + c_ref[...].astype(F32)
    scratch[...] = res_ref[...] + mixture
    gather_rows(scratch, out_ref, images, stride)


def finish(residual, pieces, tokens, images, stride):
    return pl.pallas_call(
        functools.partial(finish_kernel, images, stride),
        out_shape=sds((tokens, residual.shape[1]), F32),
        in_specs=[vmem_spec()] * 4,
        out_specs=vmem_spec(),
        scratch_shapes=[pltpu.VMEM(residual.shape, F32)],
        compiler_params=params(24),
        cost_estimate=cost(2),
        name="finish_rows",
    )(residual, *pieces)


def body(
    sizes,
    block_input,
    cotangent,
    query_weight,
    key_weight,
    value_weight,
    output_weight,
    first_gain,
    first_shift,
    expert_in,
    expert_out,
    second_gain,
    second_shift,
    routes,
    route_gates,
    clip_threshold,
):
    dp, tensor = sizes["dp"], sizes["tensor"]
    inner = dp // OUTER
    tokens, features = block_input.shape
    columns = query_weight.shape[1]
    heads = columns // HD
    images = tokens // SEQ
    stride = up(SEQ, 8)
    padded = up(images * stride, 16)
    experts = expert_in.shape[0]
    mine = experts // 2
    half = mine // 2
    block = features // OUTER
    limit = 2 * CAP
    dp_at = lax.axis_index("dp")
    place = dp_at // inner
    tensor_at = lax.axis_index("tensor")
    low_bit = place >> 1 & 1

    def along(axis, size, flip):
        pairs = [(i, i ^ flip) for i in range(size)]
        return lambda value: lax.ppermute(value, axis, pairs)

    send_x = along("dp", dp, 1 * inner)
    send_low = along("dp", dp, 2 * inner)
    send_high = along("dp", dp, 4 * inner)
    send_core = along("tensor", tensor, 1)
    send_y = along("tensor", tensor, 2)

    def whole_block(value, axis):
        if inner == 1:
            return value
        every = lax.all_gather(value, "dp", axis=axis, tiled=True)
        return lax.dynamic_slice_in_dim(every, place * block, block, axis)

    def own_rows(value, axis):
        if inner == 1:
            return value
        shape = list(value.shape)
        shape[axis] = features
        every = lax.dynamic_update_slice_in_dim(jnp.zeros(shape, value.dtype), value, place * block, axis)
        return lax.psum_scatter(every, "dp", scatter_dimension=axis, tiled=True)

    packed = jnp.concatenate(
        (output_weight.T, query_weight, key_weight, value_weight), 1
    ).astype(BF16)
    packed = whole_block(packed, 0)
    norms = jnp.stack((first_gain, first_shift, second_gain, second_shift)).astype(BF16)
    norms = whole_block(norms, 1)
    norms = lax.dynamic_update_slice(jnp.zeros((EXTRA, features), BF16), norms, (0, place * block))
    own = jnp.concatenate((packed, norms), 0)[None]
    cot_half = spread(cotangent, images, stride, padded)
    cot_y = send_y(cot_half)
    pair = jnp.concatenate((own, send_high(own)), 0)
    four = jnp.concatenate((pair, send_low(pair)), 0)
    four_x, four_y = send_x(four), send_y(four)
    cot_low = send_low(after(cot_half, four))

    w_in = whole_block(expert_in.astype(BF16), 1)
    w_out = whole_block(expert_out.astype(BF16), 2).swapaxes(1, 2)
    both = jnp.stack((w_in, w_out), 1)
    w_keep = lax.dynamic_slice_in_dim(both, low_bit * mine, mine, 0)
    w_give = lax.dynamic_slice_in_dim(both, (1 - low_bit) * mine, mine, 0)
    w_high_first = send_high(after(w_keep[:1], four))
    w_high_rest = send_high(after(w_keep[1:3], w_high_first))

    eight = jnp.concatenate((four, four_x), 0)
    two_a, two_b = send_x(after(four_y[:2], w_high_first)), send_y(four_x[2:])
    eight_y = after(jnp.concatenate((four_y, two_a, two_b), 0), cot_low)
    pieces = [eight, eight_y, send_core(eight), send_core(eight_y)]
    flips = tuple(block_flip(x_bit, low, high) for x_bit in (0, 1) for low in (0, 1) for high in (0, 1))
    layout = [tuple((t, flip) for flip in flips) for t in range(4)]
    gains = jnp.sum(eight[:, block:].astype(F32), 0)
    w_low = send_low(after(w_give, cot_low))
    cot_far = send_y(cot_low)
    w_keep_x = send_x(after(w_keep, two_a))

    table = jnp.concatenate((routes.T.astype(F32), route_gates.T), 0)
    picks = routes.shape[1]
    table = table.reshape(2 * picks, tensor, images, SEQ)
    table = jnp.pad(table, ((0, 0), (0, 0), (0, 0), (0, stride - SEQ)), constant_values=-1)
    table = table.reshape(2 * picks, tensor, images * stride)
    table = jnp.pad(table, ((0, 0), (0, 0), (0, padded - images * stride)), constant_values=-1)
    table = jnp.stack((table, send_low(table)))
    table = table.reshape(2, 2 * picks, 2, 2, padded)
    table = jnp.where(tensor_at >> 1 & 1 == 1, table[:, :, ::-1], table)
    table = jnp.where(tensor_at & 1 == 1, table[:, :, :, ::-1], table)
    table = table.transpose(1, 3, 0, 2, 4).reshape(2 * picks, 8, padded)
    ids = (low_bit * mine + jnp.arange(mine)).astype(F32)[None, :, None, None]
    hits = table[:picks, None] == ids
    chosen = jnp.any(hits, 0)
    gates = jnp.sum(jnp.where(hits, table[picks:, None], 0.0), 0)
    order = lax.broadcasted_iota(jnp.int32, (padded, padded), 0) < lax.broadcasted_iota(
        jnp.int32, (padded, padded), 1
    )
    before = jnp.dot(
        chosen.reshape(-1, padded).astype(BF16), order.astype(BF16), preferred_element_type=F32
    ).reshape(chosen.shape)
    counts = jnp.sum(chosen.astype(F32), -1)
    ahead = (jnp.arange(8)[:, None] < jnp.arange(8)[None, :]).astype(F32)
    starts = jnp.sum(counts[:, :, None] * ahead[None], 1)
    slots = jnp.where(chosen, starts[:, :, None] + before, -1.0).astype(jnp.int32)
    totals = jnp.sum(counts, 1)
    scalars = jnp.concatenate((starts.reshape(-1), counts.reshape(-1), totals)).astype(jnp.int32)
    slot_columns = slots.transpose(1, 2, 0)
    gate_columns = gates.transpose(1, 2, 0)

    place_word = place.astype(jnp.int32).reshape(1)
    residual, second, first, weights, kept, peaks = attention_forward(
        after(place_word, scalars, slots, gates, slot_columns, gate_columns), block_input, gains, pieces, layout, images, stride, padded, tensor, heads
    )
    second, w_low, w_high_rest, w_keep_x, cot_far = lax.optimization_barrier(
        (second, w_low, w_high_rest, w_keep_x, cot_far)
    )
    w_high_last = send_high(after(w_keep[3:], w_high_rest))

    by_low, by_y = send_low(second), send_y(second)
    w_low_x = send_x(w_low)
    cot_shards = jnp.stack((cot_half, cot_y, cot_low, cot_far))
    cot_slots = dispatch(scalars, (cot_shards, send_core(cot_shards)), slots, gates, limit)
    w_low_0 = send_high(after(w_low[:half], second))
    cot_slots, by_low, by_y, w_low_x, w_high_last = lax.optimization_barrier(
        (cot_slots, by_low, by_y, w_low_x, w_high_last)
    )
    w_high = jnp.concatenate((w_high_first, w_high_rest, w_high_last), 0)
    by_far = send_y(by_low)
    shards = [second, by_y, by_low, by_far]
    shards += [send_core(piece) for piece in shards]
    w_high_x = send_x(after(w_high, w_low_x))
    w_low_1 = send_high(after(w_low[half:], by_low))
    w_low_x_0 = send_x(after(w_low_0, w_high_x))
    x_slots = dispatch(after(scalars, w_low_0), shards, slots, None, limit)
    w_low_1 = after(w_low_1, x_slots)
    w_low_x_1 = send_x(w_low_1)

    def run_experts(c, x, weights):
        info = jnp.concatenate((place_word, totals[c * half : (c + 1) * half].astype(jnp.int32)))
        return expert_math(info, x, cot_slots, weights, c * half, half, limit)

    basic = (w_keep, w_low, w_high)
    basic_x = (w_keep_x, w_low_x, w_high_x)
    y_0, dx_0, *shares_0 = run_experts(0, after(x_slots, w_low_1), (*basic, w_low_0, *basic_x, w_low_x_0))
    keep_0, give_0 = shares_0[:2], shares_0[2:]
    give_0[0], x_slots = lax.optimization_barrier((give_0[0], x_slots, w_low_x_1))[:2]
    side_in_0 = send_x(give_0[0])
    y_1, dx_1, *shares_1 = run_experts(1, x_slots, (*basic, w_low_1, *basic_x, w_low_x_1))
    keep_1, give_1 = shares_1[:2], shares_1[2:]
    dx_1 = after(dx_1, side_in_0)
    side_out_0 = send_x(after(give_0[1], dx_1))
    rows = keep_0[0].shape[1] // 2

    def upper_sum(keep, side):
        return keep[:, rows:] + side[:, rows:]

    def lower_sum(keep, side, high):
        return (keep[:, :rows].astype(F32) + side[:, :rows].astype(F32) + high.astype(F32)).astype(BF16)

    high_in_0 = send_high(after(upper_sum(keep_0[0], side_in_0), dx_1))
    give, hold = combine(scalars, (dx_0, dx_1), slot_columns, None)
    give, side_out_0 = lax.optimization_barrier((give, side_out_0))
    core = send_core(give)
    core, high_in_0 = lax.optimization_barrier((core, high_in_0))
    high_out_0 = send_high(after(upper_sum(keep_0[1], side_out_0), give))
    sums = [hold[i] + core[i] for i in range(4)]
    far_y, near_y = send_y(sums[3]), send_y(sums[1])
    side_in_1 = send_x(after(give_1[0], give))
    give, hold_y = combine(after(scalars, sums[3]), (y_0, y_1), slot_columns, gate_columns)
    give, side_in_1, far_y, high_out_0 = lax.optimization_barrier((give, side_in_1, far_y, high_out_0))
    core_y = send_core(give)
    low = send_low(sums[2] + far_y)
    side_out_1 = send_x(after(give_1[1], give))
    mixture = [hold_y[i] + core_y[i] for i in range(4)]
    mixture_y = send_y(jnp.stack((mixture[1], mixture[3])))
    high_in_1 = send_high(after(upper_sum(keep_1[0], side_in_1), high_out_0))
    high_out_1 = send_high(after(upper_sum(keep_1[1], side_out_1), high_out_0))
    grad_pieces = (after(sums[0], *mixture, side_out_1), near_y, low)
    mine_0 = jnp.stack(
        (lower_sum(keep_0[0], side_in_0, high_in_0), lower_sum(keep_0[1], side_out_0, high_out_0)), 1
    )
    low_0 = send_low(mine_0[:, :, block:])

    peak = peaks[:, 0, :heads].reshape(2, 2, heads)
    peak = jnp.where(tensor_at & 1 == 1, peak[::-1], peak)
    peak = jnp.where(tensor_at >> 1 & 1 == 1, peak[:, ::-1], peak)
    peak = peak.transpose(1, 0, 2).reshape(tensor * heads)
    extra = jnp.zeros((EXTRA, features), F32)
    if inner == 1:
        device = dp_at * tensor + tensor_at
        high = lax.reduce_precision(peak, 8, 7)
        rest = lax.reduce_precision(peak - high, 8, 7)
        is_mine = (jnp.arange(dp * tensor) == device)[None, :, None]
        words = jnp.where(is_mine, jnp.stack((high, rest))[:, None, :], 0.0).reshape(2, -1)
        extra = extra.at[4:6, : words.shape[1]].set(words)
    weights = weights.reshape(2, 2, features, features)
    kept = kept.reshape(2, 2, padded, features)
    keep_b, send_b, resid, dattn, total, firsts, halves, extra = attention_backward(
        cotangent, residual, grad_pieces, first, weights, kept, gains, extra, images, stride, heads
    )
    total, send_b, mixture_y, high_in_1, low_0 = lax.optimization_barrier(
        (total, send_b, mixture_y, high_in_1, low_0)
    )
    upper = send_y(keep_b + send_core(send_b))
    mixture_low = send_low(mixture[2] + mixture_y[1])
    input_grad, keep, send, extra = attention_rest(
        block_input, resid, dattn, total, firsts, halves, weights, kept, gains, extra, images, stride, heads
    )
    send, extra, upper, high_out_1, mixture_low = lax.optimization_barrier(
        (send, extra, upper, high_out_1, mixture_low)
    )
    mine_1 = jnp.stack(
        (lower_sum(keep_1[0], side_in_1, high_in_1), lower_sum(keep_1[1], side_out_1, high_out_1)), 1
    )
    low_1 = send_low(mine_1[:, :, block:])

    near = send_core(send)
    extra_y = send_y(extra)
    extra_far = lax.ppermute(extra, "tensor", [(i, i ^ 3) for i in range(tensor)])
    others = jnp.broadcast_to(extra_y.astype(F32) + extra_far.astype(F32), (OUTER, EXTRA, features))
    others = jnp.concatenate((upper.astype(F32), others), 1)
    total = (keep.astype(F32) + near.astype(F32) + others).astype(BF16)
    total, low_1 = lax.optimization_barrier((total, low_1))
    block_output = finish(residual, (mixture[0], mixture_y[0], mixture_low), tokens, images, stride)

    own_share = jnp.concatenate((mine_0[:, :, :block], mine_1[:, :, :block]), 0)
    far_share = jnp.concatenate((low_0, low_1), 0)
    grads = jnp.concatenate(
        (
            jnp.where(low_bit == 0, own_share, far_share),
            jnp.where(low_bit == 0, far_share, own_share),
        ),
        0,
    ).astype(F32)
    expert_in_grad = own_rows(grads[:, 0], 1)
    expert_out_grad = own_rows(grads[:, 1].swapaxes(1, 2), 2)

    if inner == 1:
        total = lax.all_to_all(total, "dp", 0, 0, tiled=True)
        total = jnp.sum(total.astype(F32), 0)
        words = total[block:]
        total = total[:block]
        peak = jnp.sum(words[4:6, : dp * tensor * tensor * heads], 0).reshape(dp * tensor, tensor * heads)
        peak = jnp.max(peak, 0)
    else:
        words = lax.psum(total[0, block:].astype(F32), "dp")
        total = total[:, :block].reshape(features, features).astype(F32)
        total = lax.psum_scatter(total, "dp", scatter_dimension=0, tiled=True)
        peak = lax.pmax(peak, ("dp", "tensor"))
    head_maxima = lax.dynamic_slice_in_dim(peak, tensor_at * heads, heads, 0)
    vectors = lax.dynamic_slice_in_dim(words[:4], dp_at * (features // dp), features // dp, 1)
    output_grad, query_grad, key_grad, value_grad = (
        total[:, i * columns : (i + 1) * columns] for i in range(4)
    )
    factor = jnp.minimum(1.0, clip_threshold / jnp.maximum(head_maxima, 1.0))
    column_scale = jnp.repeat(jnp.sqrt(factor), HD)
    return (
        block_output,
        input_grad,
        query_grad,
        key_grad,
        value_grad,
        output_grad.T,
        vectors[0],
        vectors[1],
        expert_in_grad,
        expert_out_grad,
        vectors[2],
        vectors[3],
        query_weight * column_scale[None, :],
        key_weight * column_scale[None, :],
        head_maxima,
    )


def solution(mesh):
    rows = P(("dp", "tensor"), None)
    by_column, by_row, by_dp = P("dp", "tensor"), P("tensor", "dp"), P("dp")
    up_spec, down_spec = P(None, "dp", "tensor"), P(None, "tensor", "dp")
    sizes = dict(mesh.shape)
    return jax.shard_map(
        functools.partial(body, sizes),
        mesh=mesh,
        in_specs=(
            rows, rows, by_column, by_column, by_column, by_row, by_dp, by_dp, up_spec, down_spec,
            by_dp, by_dp, P("dp", None), P("dp", None), P("tensor"),
        ),
        out_specs=(
            rows, rows, by_column, by_column, by_column, by_row, by_dp, by_dp, up_spec, down_spec,
            by_dp, by_dp, by_column, by_column, P("tensor"),
        ),
        check_vma=False,
    )
```

```python
import functools
import math

import jax
import jax.numpy as jnp
from jax import lax
from jax.experimental import pallas as pl
from jax.experimental.pallas import tpu as pltpu
from jax.sharding import PartitionSpec as P

HD = 64
SEQ = 197
CAP = 792
EPSILON = 1e-06
F32 = jnp.float32
BF16 = jnp.bfloat16
OUTER = 8
EXTRA = 16
ROW_TILE = 256
WINDOW = 256
MIB = 1 << 20


def up(number, unit):
    return -(-number // unit) * unit


def dot(left, right, contract=((1,), (0,))):
    return lax.dot_general(left, right, (contract, ((), ())), preferred_element_type=F32)


def params(mib):
    return pltpu.CompilerParams(vmem_limit_bytes=mib * MIB)


def any_spec():
    return pl.BlockSpec(memory_space=pl.ANY)


def vmem_spec():
    return pl.BlockSpec(memory_space=pltpu.VMEM)


def smem_spec():
    return pl.BlockSpec(memory_space=pltpu.SMEM)


def sds(shape, dtype):
    return jax.ShapeDtypeStruct(shape, dtype)


def cost(microseconds):
    return pl.CostEstimate(flops=int(microseconds * 0.5e9), bytes_accessed=0, transcendentals=0)


def after(value, *others):
    return lax.optimization_barrier((value, *others))[0]


def block_flip(x_bit, low_bit, high_bit):
    return x_bit | low_bit << 1 | high_bit << 2


def norm_stats(values):
    mean = jnp.mean(values, -1, keepdims=True)
    centred = values - mean
    scale = lax.rsqrt(jnp.mean(centred * centred, -1, keepdims=True) + EPSILON)
    return centred * scale, scale


def spread_rows(source, target, images, stride):
    for i in range(images):
        target[i * stride : i * stride + SEQ, :] = source[i * SEQ : (i + 1) * SEQ, :].astype(F32)
        end = (i + 1) * stride if i + 1 < images else target.shape[0]
        target[i * stride + SEQ : end, :] = jnp.zeros((end - i * stride - SEQ, target.shape[1]), F32)


def gather_rows(source, target, images, stride):
    for i in range(images):
        target[i * SEQ : (i + 1) * SEQ, :] = source[i * stride : i * stride + SEQ, :]


def attention_forward_kernel(images, stride, heads, layout, *refs):
    n_pieces = len(layout)
    place_ref, x_ref, gains_ref = refs[:3]
    piece_refs = refs[3 : 3 + n_pieces]
    res_ref, second_ref, first_ref, w_ref, kept_ref, peak_ref = refs[3 + n_pieces : 9 + n_pieces]
    scratch, sems = refs[9 + n_pieces :]
    columns = heads * HD
    block = w_ref.shape[1] // OUTER
    place = place_ref[0]
    copies = []
    for ref, entries in zip(piece_refs, layout):
        for j, (t, flip) in enumerate(entries):
            row = pl.multiple_of((place ^ flip) * block, 16)
            copies.append(
                pltpu.make_async_copy(
                    ref.at[j, pl.ds(0, block), :],
                    w_ref.at[t, pl.ds(row, block), :],
                    sems.at[len(copies)],
                )
            )
            copies[-1].start()
    spread_rows(x_ref, res_ref, images, stride)
    unit, _ = norm_stats(res_ref[...])
    first_ref[...] = (unit * gains_ref[0:1, :] + gains_ref[1:2, :]).astype(BF16)
    for copy in copies:
        copy.wait()
    scale = 1.0 / math.sqrt(HD)
    key_ok = lax.broadcasted_iota(jnp.int32, (stride, stride), 0) < SEQ
    query_ok = lax.broadcasted_iota(jnp.int32, (1, stride), 1) < SEQ
    lane = lax.broadcasted_iota(jnp.int32, (8, 128), 1)

    def step(t, carry):
        scratch[...] = dot(first_ref[...], w_ref[t]).astype(BF16).astype(F32)
        peaks = jnp.full((8, 128), -jnp.inf, F32)
        for i in range(images):
            rows = slice(i * stride, (i + 1) * stride)
            for h in range(heads):
                at = [slice((1 + p) * columns + h * HD, (1 + p) * columns + (h + 1) * HD) for p in range(3)]
                q = (scratch[rows, at[0]] * scale).astype(BF16)
                k = scratch[rows, at[1]].astype(BF16)
                v = scratch[rows, at[2]].astype(BF16)
                s = jnp.where(key_ok, dot(k, q, ((1,), (1,))), -1e30)
                top = jnp.max(s, 0, keepdims=True)
                e = jnp.exp(s - top)
                p = e * (1.0 / jnp.sum(e, 0, keepdims=True))
                o = dot(v, p.astype(BF16), ((0,), (0,))).T
                scratch[rows, h * HD : (h + 1) * HD] = o.astype(BF16).astype(F32)
                peak = jnp.max(jnp.where(query_ok, top, -jnp.inf), keepdims=True)
                peaks = jnp.maximum(peaks, jnp.where(lane == h, peak, -jnp.inf))
        peak_ref[t] = peaks
        kept_ref[t] = scratch[...].astype(BF16)
        res_ref[...] += dot(kept_ref[t, :, 0:columns], w_ref[t, :, 0:columns], ((1,), (1,)))
        return carry

    lax.fori_loop(0, w_ref.shape[0], step, 0)
    unit, _ = norm_stats(res_ref[...])
    second_ref[...] = (unit * gains_ref[2:3, :] + gains_ref[3:4, :]).astype(BF16)


def attention_forward(place, rows, gains, pieces, layout, images, stride, padded, parts, heads):
    features = rows.shape[1]
    n_copies = sum(len(entries) for entries in layout)
    return pl.pallas_call(
        functools.partial(attention_forward_kernel, images, stride, heads, layout),
        out_shape=(
            sds((padded, features), F32),
            sds((padded, features), BF16),
            sds((padded, features), BF16),
            sds((parts, features, features), BF16),
            sds((parts, padded, features), BF16),
            sds((parts, 8, 128), F32),
        ),
        in_specs=[smem_spec(), vmem_spec(), vmem_spec()] + [any_spec()] * len(pieces),
        out_specs=(vmem_spec(),) * 6,
        scratch_shapes=[
            pltpu.VMEM((padded, features), F32),
            pltpu.SemaphoreType.DMA((n_copies,)),
        ],
        compiler_params=params(48),
        cost_estimate=cost(22),
        name="attention_forward",
    )(place, rows, gains, *pieces)


def head_at(columns, part, head):
    return slice(part * columns + head * HD, part * columns + (head + 1) * HD)


def norm_back(grad, gain, unit, scale):
    weighted = grad * gain
    mean = jnp.mean(weighted, -1, keepdims=True)
    return (weighted - mean - unit * jnp.mean(weighted * unit, -1, keepdims=True)) * scale


def heads_backward(images, stride, heads, t, w_ref, kept_ref, half_ref, firsts, halves, kept, mixed, grads, total):
    columns = heads * HD
    features = w_ref.shape[2]
    scale = 1.0 / math.sqrt(HD)
    key_ok = lax.broadcasted_iota(jnp.int32, (stride, stride), 0) < SEQ
    kept[...] = kept_ref[t, 0].astype(F32)
    mixed[...] = dot(half_ref[...], w_ref[t, 0, :, 0:columns]).astype(BF16).astype(F32)
    for i in range(images):
        rows = slice(i * stride, (i + 1) * stride)
        for h in range(heads):
            q = (kept[rows, head_at(columns, 1, h)] * scale).astype(BF16)
            k = kept[rows, head_at(columns, 2, h)].astype(BF16)
            v = kept[rows, head_at(columns, 3, h)].astype(BF16)
            do = mixed[rows, h * HD : (h + 1) * HD].astype(BF16)
            s = jnp.where(key_ok, dot(k, q, ((1,), (1,))), -1e30)
            e = jnp.exp(s - jnp.max(s, 0, keepdims=True))
            p = e * (1.0 / jnp.sum(e, 0, keepdims=True))
            dp = dot(v, do, ((1,), (1,)))
            dv = dot(p.astype(BF16), do)
            ds = (p * (dp - jnp.sum(p * dp, 0, keepdims=True))).astype(BF16)
            dq = dot(k, ds, ((0,), (0,))).T * scale
            dk = dot(ds, q)
            grads[rows, head_at(columns, 1, h)] = dq
            grads[rows, head_at(columns, 2, h)] = dk
            grads[rows, head_at(columns, 3, h)] = dv
    packed = grads[...].astype(BF16)
    total[...] += dot(packed, w_ref[t, 0], ((1,), (1,)))
    full = dot(firsts[...], packed)
    out = dot(halves[...], kept_ref[t, 0, :, 0:columns])
    full = full + jnp.concatenate((out, jnp.zeros((features, features - columns), F32)), 1)
    return full.astype(BF16)


def half_spec(value, y):
    return pl.BlockSpec((2, 1) + value.shape[2:], lambda i: (0, y, 0, 0))


def put_blocks(refs, t, full):
    block = full.shape[0] // OUTER
    for i, ref in enumerate(refs):

        @pl.when(t == i)
        def _(ref=ref):
            for j in range(OUTER):
                ref[j, 0:block, :] = full[j * block : (j + 1) * block, :]


def attention_backward_kernel(images, stride, heads, *refs):
    (cot_ref, res_ref, d0_ref, d1_ref, d2_ref, first_ref, w_ref, kept_ref, gains_ref, extra_ref) = refs[:10]
    keep_ref, send_ref, resid, half, total, firsts, halves, more_ref = refs[10:18]
    kept, grads, mixed = refs[18:]
    features = w_ref.shape[2]
    unit, scale_two = norm_stats(res_ref[...])
    da2 = d0_ref[...].astype(F32) + d1_ref[...].astype(F32) + d2_ref[...].astype(F32)
    row = lax.broadcasted_iota(jnp.int32, (EXTRA, features), 0)
    extra = jnp.where(row == 2, jnp.sum(da2 * unit, 0, keepdims=True), extra_ref[...])
    more_ref[...] = jnp.where(row == 3, jnp.sum(da2, 0, keepdims=True), extra)
    spread_rows(cot_ref, resid, images, stride)
    resid[...] += norm_back(da2, gains_ref[2:3, :], unit, scale_two)
    half[...] = resid[...].astype(BF16)
    firsts[...] = first_ref[...].T
    halves[...] = half[...].T
    total[...] = jnp.zeros_like(total)
    grads[...] = jnp.zeros_like(grads)

    def step(t, carry):
        full = heads_backward(
            images, stride, heads, t, w_ref, kept_ref, half, firsts, halves, kept, mixed, grads, total
        )
        put_blocks((keep_ref, send_ref), t, full)
        return carry

    lax.fori_loop(0, 2, step, 0)


def attention_rest_kernel(images, stride, heads, *refs):
    (x_ref, resid_ref, half, total_ref, firsts, halves, w_ref, kept_ref, gains_ref, more_ref) = refs[:10]
    input_grad_ref, keep_ref, send_ref, extra_ref = refs[10:14]
    kept, grads, mixed, total = refs[14:]
    features = w_ref.shape[2]
    block = features // OUTER
    total[...] = total_ref[...]
    grads[...] = jnp.zeros_like(grads)

    def step(t, carry):
        full = heads_backward(
            images, stride, heads, t, w_ref, kept_ref, half, firsts, halves, kept, mixed, grads, total
        )
        put_blocks((keep_ref, send_ref), t, full)
        return carry

    lax.fori_loop(0, 2, step, 0)
    spread_rows(x_ref, kept, images, stride)
    unit, scale_one = norm_stats(kept[...])
    da = total[...]
    grads[...] = resid_ref[...] + norm_back(da, gains_ref[0:1, :], unit, scale_one)
    gather_rows(grads, input_grad_ref, images, stride)
    row = lax.broadcasted_iota(jnp.int32, (EXTRA, features), 0)
    extra = jnp.where(row == 0, jnp.sum(da * unit, 0, keepdims=True), more_ref[...])
    extra = jnp.where(row == 1, jnp.sum(da, 0, keepdims=True), extra).astype(BF16)
    extra_ref[...] = extra
    for ref in (keep_ref, send_ref):
        for j in range(OUTER):
            ref[j, block : block + EXTRA, :] = extra


def attention_backward(cot, residual, pieces, first, weights, kept, gains, extra, images, stride, heads):
    padded, features = first.shape
    share = sds((OUTER, features // OUTER, features), BF16)
    wide, half, turned = sds((padded, features), F32), sds((padded, features), BF16), sds((features, padded), BF16)
    return pl.pallas_call(
        functools.partial(attention_backward_kernel, images, stride, heads),
        grid=(1,),
        out_shape=(share, share, wide, half, wide, turned, turned, sds((EXTRA, features), F32)),
        in_specs=[vmem_spec()] * 6 + [half_spec(weights, 1), half_spec(kept, 1)] + [vmem_spec()] * 2,
        out_specs=(vmem_spec(),) * 8,
        scratch_shapes=[
            pltpu.VMEM((padded, features), F32),
            pltpu.VMEM((padded, features), F32),
            pltpu.VMEM((padded, heads * HD), F32),
        ],
        compiler_params=params(50),
        cost_estimate=cost(20),
        name="attention_backward",
    )(cot, residual, *pieces, first, weights, kept, gains, extra)


def attention_rest(rows, resid, half, total, firsts, halves, weights, kept, gains, more, images, stride, heads):
    padded, features = resid.shape
    share = sds((OUTER, features // OUTER + EXTRA, features), BF16)
    return pl.pallas_call(
        functools.partial(attention_rest_kernel, images, stride, heads),
        grid=(1,),
        out_shape=(sds(rows.shape, F32), share, share, sds((EXTRA, features), BF16)),
        in_specs=[vmem_spec()] * 6 + [half_spec(weights, 0), half_spec(kept, 0)] + [vmem_spec()] * 2,
        out_specs=(vmem_spec(),) * 4,
        scratch_shapes=[
            pltpu.VMEM((padded, features), F32),
            pltpu.VMEM((padded, features), F32),
            pltpu.VMEM((padded, heads * HD), F32),
            pltpu.VMEM((padded, features), F32),
        ],
        compiler_params=params(50),
        cost_estimate=cost(20),
        name="attention_backward_rest",
    )(rows, resid, half, total, firsts, halves, weights, kept, gains, more)


def dispatch_kernel(gated, *refs):
    table_ref = refs[0]
    slot_ref = refs[-3] if gated else refs[-2]
    gate_ref = refs[-2] if gated else None
    out_ref = refs[-1]
    shard_refs = []
    for ref in refs[1 : -3 if gated else -2]:
        shard_refs += [ref] if len(ref.shape) == 2 else [ref.at[i] for i in range(ref.shape[0])]
    n_shards = len(shard_refs)
    expert = pl.program_id(0)
    experts = pl.num_programs(0)
    padded = shard_refs[0].shape[0]
    features = shard_refs[0].shape[1]
    count_all = table_ref[2 * n_shards * experts + expert]
    tail = pl.multiple_of(count_all // 16 * 16, 16)
    out_ref[0, pl.ds(tail, ROW_TILE + 16), :] = jnp.zeros((ROW_TILE + 16, features), BF16)
    row16 = lax.broadcasted_iota(jnp.int32, (16, 1), 0)
    rows = lax.broadcasted_iota(jnp.int32, (WINDOW, padded), 0)
    starts = [table_ref[expert * n_shards + r] for r in range(n_shards)]
    numbers = [table_ref[n_shards * experts + expert * n_shards + r] for r in range(n_shards)]
    firsts = [start // 16 * 16 for start in starts]
    steps = [
        (start - first + number + WINDOW - 1) // WINDOW
        for start, first, number in zip(starts, firsts, numbers)
    ]

    def step(r, c):
        low = pl.multiple_of(firsts[r] + c * WINDOW, 16)
        hit = slot_ref[0, r : r + 1, :] - low == rows
        chosen = jnp.where(hit, 1.0, 0.0)
        got = dot(chosen.astype(BF16), shard_refs[r][...])
        if gated:
            got = got * jnp.sum(chosen * gate_ref[0, r : r + 1, :], -1, keepdims=True)
        got = got.astype(BF16)
        before = out_ref[0, pl.ds(low, 16), :]
        out_ref[0, pl.ds(low, 16), :] = jnp.where(row16 + low < starts[r], before, got[:16])
        out_ref[0, pl.ds(low + 16, WINDOW - 16), :] = got[16:]

    short = functools.reduce(jnp.maximum, steps) <= 1

    @pl.when(short)
    def _():
        for r in range(n_shards):
            step(r, 0)

    @pl.when(jnp.logical_not(short))
    def _():
        for r in range(n_shards):

            def again(c, carry, r=r):
                step(r, c)
                return carry

            lax.fori_loop(0, steps[r], again, 0)


def slot_rows(limit):
    return up(limit, ROW_TILE) + WINDOW + 16


def dispatch(table, shards, slots, gates, limit):
    experts = slots.shape[0]
    padded, features = shards[0].shape[-2:]
    length = slot_rows(limit)
    gated = gates is not None
    per_expert = pl.BlockSpec((1,) + slots.shape[1:], lambda e: (e, 0, 0))
    return pl.pallas_call(
        functools.partial(dispatch_kernel, gated),
        grid=(experts,),
        out_shape=sds((experts, length, features), BF16),
        in_specs=[smem_spec()] + [vmem_spec()] * len(shards) + [per_expert] * (2 if gated else 1),
        out_specs=pl.BlockSpec((1, length, features), lambda e: (e, 0, 0)),
        compiler_params=params(48),
        cost_estimate=cost(15),
        name="dispatch_gated" if gated else "dispatch",
    )(table, *shards, slots, *([gates] if gated else []))


def normal_share(u):
    bell = jnp.exp(-0.5 * u * u)
    t = 1.0 / (1.0 + jnp.abs(u) * (0.3275911 / math.sqrt(2.0)))
    poly = 0.5 * 1.061405429
    for term in (-1.453152027, 1.421413741, -0.284496736, 0.254829592):
        poly = poly * t + 0.5 * term
    tail = poly * t * bell
    return jnp.where(u < 0, tail, 1.0 - tail), bell


def expert_kernel(*refs):
    info_ref, x_ref, dy_ref = refs[:3]
    w_refs = refs[3:11]
    y_ref, dx_ref = refs[11:13]
    share_refs = (refs[13:15], refs[15:17])
    w_in, w_out, g_in, g_out, hidden, slopes = refs[17:]
    place = info_ref[0]
    count = info_ref[1 + pl.program_id(0)]
    features = w_in.shape[0]
    block = features // OUTER
    for number, ref in enumerate(w_refs):
        flip = block_flip(number >> 2, number & 1, number >> 1 & 1)
        row = pl.multiple_of((place ^ flip) * block, 16)
        w_in[pl.ds(row, block), :] = ref[0, 0]
        w_out[pl.ds(row, block), :] = ref[0, 1]
    g_in[...] = jnp.zeros_like(g_in)
    g_out[...] = jnp.zeros_like(g_out)
    tiles = jnp.maximum((count + ROW_TILE - 1) // ROW_TILE, 1)

    def at(i):
        return pl.ds(pl.multiple_of(i * ROW_TILE, ROW_TILE), ROW_TILE)

    def first_half(i):
        pre = dot(x_ref[0, at(i), :], w_in[...])
        dh = dot(dy_ref[0, at(i), :], w_out[...])
        share, bell = normal_share(pre)
        hidden[i % 2] = (pre * share).astype(BF16)
        slope = share + pre * bell * (1.0 / math.sqrt(2.0 * math.pi))
        slopes[i % 2] = (dh * slope).astype(BF16)

    def second_half(i):
        hid, dpre = hidden[i % 2], slopes[i % 2]
        y_ref[0, at(i), :] = dot(hid, w_out[...], ((1,), (1,))).astype(BF16)
        dx_ref[0, at(i), :] = dot(dpre, w_in[...], ((1,), (1,))).astype(BF16)
        g_in[...] += dot(x_ref[0, at(i), :], dpre, ((0,), (0,)))
        g_out[...] += dot(dy_ref[0, at(i), :], hid, ((0,), (0,)))

    def tile(i, carry):
        second_half(i - 1)
        first_half(i)
        return carry

    first_half(0)
    lax.fori_loop(1, tiles, tile, 0)
    second_half(tiles - 1)
    rest = pl.ds(pl.multiple_of(tiles * ROW_TILE, 16), WINDOW + 16)
    y_ref[0, rest, :] = jnp.zeros((WINDOW + 16, features), BF16)
    dx_ref[0, rest, :] = jnp.zeros((WINDOW + 16, features), BF16)
    for number in range(OUTER):
        flip = block_flip(number >> 2 & 1, number & 1, number >> 1 & 1)
        row = pl.multiple_of((place ^ flip) * block, 16)
        in_ref, out_ref = share_refs[number // (OUTER // 2)]
        at = slice(number % (OUTER // 2) * block, (number % (OUTER // 2) + 1) * block)
        in_ref[0, at, :] = g_in[pl.ds(row, block), :].astype(BF16)
        out_ref[0, at, :] = g_out[pl.ds(row, block), :].astype(BF16)


def expert_math(info, x, dy, weights, first, experts, limit):
    length, features = x.shape[1:]
    hidden = weights[0].shape[3]
    most = up(limit, ROW_TILE)
    slots_spec = pl.BlockSpec((1, most, features), lambda e: (e + first, 0, 0))
    out_spec = pl.BlockSpec((1, length, features), lambda e: (e, 0, 0))
    share = sds((experts, features // 2, hidden), BF16)
    share_spec = pl.BlockSpec((1, features // 2, hidden), lambda e: (e, 0, 0))
    return pl.pallas_call(
        expert_kernel,
        grid=(experts,),
        out_shape=(sds((experts, length, features), BF16),) * 2 + (share,) * 4,
        in_specs=[smem_spec(), slots_spec, slots_spec]
        + [pl.BlockSpec((1,) + w.shape[1:], lambda e, at=first * (w.shape[0] > experts): (e + at, 0, 0, 0))
            for w in weights
],
        out_specs=(out_spec, out_spec) + (share_spec,) * 4,
        scratch_shapes=[
            pltpu.VMEM((features, hidden), BF16),
            pltpu.VMEM((features, hidden), BF16),
            pltpu.VMEM((features, hidden), F32),
            pltpu.VMEM((features, hidden), F32),
            pltpu.VMEM((2, ROW_TILE, hidden), BF16),
            pltpu.VMEM((2, ROW_TILE, hidden), BF16),
        ],
        compiler_params=params(60),
        cost_estimate=cost(33),
        name="expert_math",
    )(info, x, dy, *weights)


def combine_kernel(gated, n_sources, *refs):
    table_ref = refs[0]
    source_refs = refs[1 : 1 + n_sources]
    slot_ref = refs[1 + n_sources]
    gate_ref = refs[2 + n_sources] if gated else None
    send_ref, keep_ref, window = refs[-3:]
    r = pl.program_id(0)
    n_shards = pl.num_programs(0)
    per_source = source_refs[0].shape[0]
    experts = per_source * n_sources
    shard = lax.rem(r + n_shards // 2, n_shards)
    padded = slot_ref.shape[1]
    lanes = lax.broadcasted_iota(jnp.int32, (padded, WINDOW), 1)

    def chosen(e, low):
        hit = slot_ref[0, :, e : e + 1] == lanes + low
        return jnp.where(hit, gate_ref[0, :, e : e + 1] if gated else 1.0, 0.0).astype(BF16)

    firsts, steps, parts = [], [], []
    for e in range(experts):
        start = table_ref[e * n_shards + shard]
        number = table_ref[n_shards * experts + e * n_shards + shard]
        first = pl.multiple_of(start // 16 * 16, 16)
        firsts.append(first)
        steps.append((start - first + number + WINDOW - 1) // WINDOW)
        window[e * WINDOW : (e + 1) * WINDOW, :] = source_refs[e // per_source][e % per_source, pl.ds(first, WINDOW), :]
        parts.append(chosen(e, first))
    total = dot(jnp.concatenate(parts, 1), window[...]).astype(BF16)

    def finish(ref):
        ref[0] = total
        for e in range(experts):

            def step(c, carry, e=e):
                low = pl.multiple_of(firsts[e] + c * WINDOW, 16)
                rows = source_refs[e // per_source][e % per_source, pl.ds(low, WINDOW), :]
                ref[0] = (ref[0].astype(F32) + dot(chosen(e, low), rows)).astype(BF16)
                return carry

            lax.fori_loop(1, steps[e], step, 0)

    @pl.when(r < n_shards // 2)
    def _():
        finish(send_ref)

    @pl.when(r >= n_shards // 2)
    def _():
        finish(keep_ref)


def combine(table, sources, slots, gates):
    n_shards, padded, experts = slots.shape
    features = sources[0].shape[2]
    gated = gates is not None
    half = n_shards // 2
    per_shard = pl.BlockSpec((1, padded, experts), lambda r: (lax.rem(r + half, n_shards), 0, 0))
    share = sds((half, padded, features), BF16)
    return pl.pallas_call(
        functools.partial(combine_kernel, gated, len(sources)),
        grid=(n_shards,),
        out_shape=(share, share),
        in_specs=[smem_spec()] + [vmem_spec()] * len(sources) + [per_shard] * (2 if gated else 1),
        out_specs=(
            pl.BlockSpec((1, padded, features), lambda r: (jnp.minimum(r, half - 1), 0, 0)),
            pl.BlockSpec((1, padded, features), lambda r: (jnp.maximum(r - half, 0), 0, 0)),
        ),
        scratch_shapes=[pltpu.VMEM((experts * WINDOW, features), BF16)],
        compiler_params=params(48),
        cost_estimate=cost(2),
        name="combine_gated" if gated else "combine",
    )(table, *sources, slots, *([gates] if gated else []))


def spread_kernel(images, stride, x_ref, out_ref, scratch):
    spread_rows(x_ref, scratch, images, stride)
    out_ref[...] = scratch[...].astype(BF16)


def spread(rows, images, stride, padded):
    return pl.pallas_call(
        functools.partial(spread_kernel, images, stride),
        out_shape=sds((padded, rows.shape[1]), BF16),
        in_specs=[vmem_spec()],
        out_specs=vmem_spec(),
        scratch_shapes=[pltpu.VMEM((padded, rows.shape[1]), F32)],
        compiler_params=params(16),
        cost_estimate=cost(2),
        name="spread_rows",
    )(rows)


def finish_kernel(images, stride, res_ref, a_ref, b_ref, c_ref, out_ref, scratch):
    mixture = a_ref[...].astype(F32) + b_ref[...].astype(F32) + c_ref[...].astype(F32)
    scratch[...] = res_ref[...] + mixture
    gather_rows(scratch, out_ref, images, stride)


def finish(residual, pieces, tokens, images, stride):
    return pl.pallas_call(
        functools.partial(finish_kernel, images, stride),
        out_shape=sds((tokens, residual.shape[1]), F32),
        in_specs=[vmem_spec()] * 4,
        out_specs=vmem_spec(),
        scratch_shapes=[pltpu.VMEM(residual.shape, F32)],
        compiler_params=params(24),
        cost_estimate=cost(2),
        name="finish_rows",
    )(residual, *pieces)


def body(
    sizes,
    block_input,
    cotangent,
    query_weight,
    key_weight,
    value_weight,
    output_weight,
    first_gain,
    first_shift,
    expert_in,
    expert_out,
    second_gain,
    second_shift,
    routes,
    route_gates,
    clip_threshold,
):
    dp, tensor = sizes["dp"], sizes["tensor"]
    inner = dp // OUTER
    tokens, features = block_input.shape
    columns = query_weight.shape[1]
    heads = columns // HD
    images = tokens // SEQ
    stride = up(SEQ, 8)
    padded = up(images * stride, 16)
    experts = expert_in.shape[0]
    mine = experts // 2
    half = mine // 2
    block = features // OUTER
    limit = 2 * CAP
    dp_at = lax.axis_index("dp")
    place = dp_at // inner
    tensor_at = lax.axis_index("tensor")
    low_bit = place >> 1 & 1

    def along(axis, size, flip):
        pairs = [(i, i ^ flip) for i in range(size)]
        return lambda value: lax.ppermute(value, axis, pairs)

    send_x = along("dp", dp, 1 * inner)
    send_low = along("dp", dp, 2 * inner)
    send_high = along("dp", dp, 4 * inner)
    send_core = along("tensor", tensor, 1)
    send_y = along("tensor", tensor, 2)

    def whole_block(value, axis):
        if inner == 1:
            return value
        every = lax.all_gather(value, "dp", axis=axis, tiled=True)
        return lax.dynamic_slice_in_dim(every, place * block, block, axis)

    def own_rows(value, axis):
        if inner == 1:
            return value
        shape = list(value.shape)
        shape[axis] = features
        every = lax.dynamic_update_slice_in_dim(jnp.zeros(shape, value.dtype), value, place * block, axis)
        return lax.psum_scatter(every, "dp", scatter_dimension=axis, tiled=True)

    packed = jnp.concatenate(
        (output_weight.T, query_weight, key_weight, value_weight), 1
    ).astype(BF16)
    packed = whole_block(packed, 0)
    norms = jnp.stack((first_gain, first_shift, second_gain, second_shift)).astype(BF16)
    norms = whole_block(norms, 1)
    norms = lax.dynamic_update_slice(jnp.zeros((EXTRA, features), BF16), norms, (0, place * block))
    own = jnp.concatenate((packed, norms), 0)[None]
    cot_half = spread(cotangent, images, stride, padded)
    cot_y = send_y(cot_half)
    pair = jnp.concatenate((own, send_high(own)), 0)
    four = jnp.concatenate((pair, send_low(pair)), 0)
    four_x, four_y = send_x(four), send_y(four)
    cot_low = send_low(after(cot_half, four))

    w_in = whole_block(expert_in.astype(BF16), 1)
    w_out = whole_block(expert_out.astype(BF16), 2).swapaxes(1, 2)
    both = jnp.stack((w_in, w_out), 1)
    w_keep = lax.dynamic_slice_in_dim(both, low_bit * mine, mine, 0)
    w_give = lax.dynamic_slice_in_dim(both, (1 - low_bit) * mine, mine, 0)
    w_high_first = send_high(after(w_keep[:1], four))
    w_high_rest = send_high(after(w_keep[1:3], w_high_first))

    eight = jnp.concatenate((four, four_x), 0)
    two_a, two_b = send_x(after(four_y[:2], w_high_first)), send_y(four_x[2:])
    eight_y = after(jnp.concatenate((four_y, two_a, two_b), 0), cot_low)
    pieces = [eight, eight_y, send_core(eight), send_core(eight_y)]
    flips = tuple(block_flip(x_bit, low, high) for x_bit in (0, 1) for low in (0, 1) for high in (0, 1))
    layout = [tuple((t, flip) for flip in flips) for t in range(4)]
    gains = jnp.sum(eight[:, block:].astype(F32), 0)
    w_low = send_low(after(w_give, cot_low))
    cot_far = send_y(cot_low)
    w_keep_x = send_x(after(w_keep, two_a))

    table = jnp.concatenate((routes.T.astype(F32), route_gates.T), 0)
    picks = routes.shape[1]
    table = table.reshape(2 * picks, tensor, images, SEQ)
    table = jnp.pad(table, ((0, 0), (0, 0), (0, 0), (0, stride - SEQ)), constant_values=-1)
    table = table.reshape(2 * picks, tensor, images * stride)
    table = jnp.pad(table, ((0, 0), (0, 0), (0, padded - images * stride)), constant_values=-1)
    table = jnp.stack((table, send_low(table)))
    table = table.reshape(2, 2 * picks, 2, 2, padded)
    table = jnp.where(tensor_at >> 1 & 1 == 1, table[:, :, ::-1], table)
    table = jnp.where(tensor_at & 1 == 1, table[:, :, :, ::-1], table)
    table = table.transpose(1, 3, 0, 2, 4).reshape(2 * picks, 8, padded)
    ids = (low_bit * mine + jnp.arange(mine)).astype(F32)[None, :, None, None]
    hits = table[:picks, None] == ids
    chosen = jnp.any(hits, 0)
    gates = jnp.sum(jnp.where(hits, table[picks:, None], 0.0), 0)
    order = lax.broadcasted_iota(jnp.int32, (padded, padded), 0) < lax.broadcasted_iota(
        jnp.int32, (padded, padded), 1
    )
    before = jnp.dot(
        chosen.reshape(-1, padded).astype(BF16), order.astype(BF16), preferred_element_type=F32
    ).reshape(chosen.shape)
    counts = jnp.sum(chosen.astype(F32), -1)
    ahead = (jnp.arange(8)[:, None] < jnp.arange(8)[None, :]).astype(F32)
    starts = jnp.sum(counts[:, :, None] * ahead[None], 1)
    slots = jnp.where(chosen, starts[:, :, None] + before, -1.0).astype(jnp.int32)
    totals = jnp.sum(counts, 1)
    scalars = jnp.concatenate((starts.reshape(-1), counts.reshape(-1), totals)).astype(jnp.int32)
    slot_columns = slots.transpose(1, 2, 0)
    gate_columns = gates.transpose(1, 2, 0)

    place_word = place.astype(jnp.int32).reshape(1)
    residual, second, first, weights, kept, peaks = attention_forward(
        after(place_word, scalars, slots, gates, slot_columns, gate_columns), block_input, gains, pieces, layout, images, stride, padded, tensor, heads
    )
    second, w_low, w_high_rest, w_keep_x, cot_far = lax.optimization_barrier(
        (second, w_low, w_high_rest, w_keep_x, cot_far)
    )
    w_high_last = send_high(after(w_keep[3:], w_high_rest))

    by_low, by_y = send_low(second), send_y(second)
    w_low_x = send_x(w_low)
    cot_shards = jnp.stack((cot_half, cot_y, cot_low, cot_far))
    cot_slots = dispatch(scalars, (cot_shards, send_core(cot_shards)), slots, gates, limit)
    w_low_0 = send_high(after(w_low[:half], second))
    cot_slots, by_low, by_y, w_low_x, w_high_last = lax.optimization_barrier(
        (cot_slots, by_low, by_y, w_low_x, w_high_last)
    )
    w_high = jnp.concatenate((w_high_first, w_high_rest, w_high_last), 0)
    by_far = send_y(by_low)
    shards = [second, by_y, by_low, by_far]
    shards += [send_core(piece) for piece in shards]
    w_high_x = send_x(after(w_high, w_low_x))
    w_low_1 = send_high(after(w_low[half:], by_low))
    w_low_x_0 = send_x(after(w_low_0, w_high_x))
    x_slots = dispatch(after(scalars, w_low_0), shards, slots, None, limit)
    w_low_1 = after(w_low_1, x_slots)
    w_low_x_1 = send_x(w_low_1)

    def run_experts(c, x, weights):
        info = jnp.concatenate((place_word, totals[c * half : (c + 1) * half].astype(jnp.int32)))
        return expert_math(info, x, cot_slots, weights, c * half, half, limit)

    basic = (w_keep, w_low, w_high)
    basic_x = (w_keep_x, w_low_x, w_high_x)
    y_0, dx_0, *shares_0 = run_experts(0, after(x_slots, w_low_1), (*basic, w_low_0, *basic_x, w_low_x_0))
    keep_0, give_0 = shares_0[:2], shares_0[2:]
    give_0[0], x_slots = lax.optimization_barrier((give_0[0], x_slots, w_low_x_1))[:2]
    side_in_0 = send_x(give_0[0])
    y_1, dx_1, *shares_1 = run_experts(1, x_slots, (*basic, w_low_1, *basic_x, w_low_x_1))
    keep_1, give_1 = shares_1[:2], shares_1[2:]
    dx_1 = after(dx_1, side_in_0)
    side_out_0 = send_x(after(give_0[1], dx_1))
    rows = keep_0[0].shape[1] // 2

    def upper_sum(keep, side):
        return keep[:, rows:] + side[:, rows:]

    def lower_sum(keep, side, high):
        return (keep[:, :rows].astype(F32) + side[:, :rows].astype(F32) + high.astype(F32)).astype(BF16)

    high_in_0 = send_high(after(upper_sum(keep_0[0], side_in_0), dx_1))
    give, hold = combine(scalars, (dx_0, dx_1), slot_columns, None)
    give, side_out_0, high_in_0 = lax.optimization_barrier((give, side_out_0, high_in_0))
    core = send_core(give)
    high_out_0 = send_high(after(upper_sum(keep_0[1], side_out_0), give))
    sums = [hold[i] + core[i] for i in range(4)]
    far_y, near_y = send_y(sums[3]), send_y(sums[1])
    side_in_1 = send_x(after(give_1[0], give))
    give, hold_y = combine(after(scalars, sums[3]), (y_0, y_1), slot_columns, gate_columns)
    give, side_in_1, far_y, high_out_0 = lax.optimization_barrier((give, side_in_1, far_y, high_out_0))
    core_y = send_core(give)
    low = send_low(sums[2] + far_y)
    side_out_1 = send_x(after(give_1[1], give))
    mixture = [hold_y[i] + core_y[i] for i in range(4)]
    mixture_y = send_y(jnp.stack((mixture[1], mixture[3])))
    high_in_1 = send_high(after(upper_sum(keep_1[0], side_in_1), high_out_0))
    high_out_1 = send_high(after(upper_sum(keep_1[1], side_out_1), high_out_0))
    grad_pieces = (after(sums[0], *mixture), near_y, low)
    mine_0 = jnp.stack(
        (lower_sum(keep_0[0], side_in_0, high_in_0), lower_sum(keep_0[1], side_out_0, high_out_0)), 1
    )
    low_0 = send_low(mine_0[:, :, block:])

    peak = peaks[:, 0, :heads].reshape(2, 2, heads)
    peak = jnp.where(tensor_at & 1 == 1, peak[::-1], peak)
    peak = jnp.where(tensor_at >> 1 & 1 == 1, peak[:, ::-1], peak)
    peak = peak.transpose(1, 0, 2).reshape(tensor * heads)
    extra = jnp.zeros((EXTRA, features), F32)
    if inner == 1:
        device = dp_at * tensor + tensor_at
        high = lax.reduce_precision(peak, 8, 7)
        rest = lax.reduce_precision(peak - high, 8, 7)
        is_mine = (jnp.arange(dp * tensor) == device)[None, :, None]
        words = jnp.where(is_mine, jnp.stack((high, rest))[:, None, :], 0.0).reshape(2, -1)
        extra = extra.at[4:6, : words.shape[1]].set(words)
    weights = weights.reshape(2, 2, features, features)
    kept = kept.reshape(2, 2, padded, features)
    keep_b, send_b, resid, dattn, total, firsts, halves, extra = attention_backward(
        cotangent, residual, grad_pieces, first, weights, kept, gains, extra, images, stride, heads
    )
    total, send_b, mixture_y, high_in_1, low_0, side_out_1 = lax.optimization_barrier(
        (total, send_b, mixture_y, high_in_1, low_0, side_out_1)
    )
    upper = send_y(keep_b + send_core(send_b))
    mixture_low = send_low(mixture[2] + mixture_y[1])
    input_grad, keep, send, extra = attention_rest(
        block_input, resid, dattn, total, firsts, halves, weights, kept, gains, extra, images, stride, heads
    )
    send, extra, upper, high_out_1, mixture_low = lax.optimization_barrier(
        (send, extra, upper, high_out_1, mixture_low)
    )
    mine_1 = jnp.stack(
        (lower_sum(keep_1[0], side_in_1, high_in_1), lower_sum(keep_1[1], side_out_1, high_out_1)), 1
    )
    low_1 = send_low(mine_1[:, :, block:])

    near = send_core(send)
    extra_y = send_y(extra)
    extra_far = lax.ppermute(extra, "tensor", [(i, i ^ 3) for i in range(tensor)])
    others = jnp.broadcast_to(extra_y.astype(F32) + extra_far.astype(F32), (OUTER, EXTRA, features))
    others = jnp.concatenate((upper.astype(F32), others), 1)
    total = (keep.astype(F32) + near.astype(F32) + others).astype(BF16)
    total, low_1 = lax.optimization_barrier((total, low_1))
    block_output = finish(residual, (mixture[0], mixture_y[0], mixture_low), tokens, images, stride)

    own_share = jnp.concatenate((mine_0[:, :, :block], mine_1[:, :, :block]), 0)
    far_share = jnp.concatenate((low_0, low_1), 0)
    grads = jnp.concatenate(
        (
            jnp.where(low_bit == 0, own_share, far_share),
            jnp.where(low_bit == 0, far_share, own_share),
        ),
        0,
    ).astype(F32)
    expert_in_grad = own_rows(grads[:, 0], 1)
    expert_out_grad = own_rows(grads[:, 1].swapaxes(1, 2), 2)

    if inner == 1:
        total = lax.all_to_all(total, "dp", 0, 0, tiled=True)
        total = jnp.sum(total.astype(F32), 0)
        words = total[block:]
        total = total[:block]
        peak = jnp.sum(words[4:6, : dp * tensor * tensor * heads], 0).reshape(dp * tensor, tensor * heads)
        peak = jnp.max(peak, 0)
    else:
        words = lax.psum(total[0, block:].astype(F32), "dp")
        total = total[:, :block].reshape(features, features).astype(F32)
        total = lax.psum_scatter(total, "dp", scatter_dimension=0, tiled=True)
        peak = lax.pmax(peak, ("dp", "tensor"))
    head_maxima = lax.dynamic_slice_in_dim(peak, tensor_at * heads, heads, 0)
    vectors = lax.dynamic_slice_in_dim(words[:4], dp_at * (features // dp), features // dp, 1)
    output_grad, query_grad, key_grad, value_grad = (
        total[:, i * columns : (i + 1) * columns] for i in range(4)
    )
    factor = jnp.minimum(1.0, clip_threshold / jnp.maximum(head_maxima, 1.0))
    column_scale = jnp.repeat(jnp.sqrt(factor), HD)
    return (
        block_output,
        input_grad,
        query_grad,
        key_grad,
        value_grad,
        output_grad.T,
        vectors[0],
        vectors[1],
        expert_in_grad,
        expert_out_grad,
        vectors[2],
        vectors[3],
        query_weight * column_scale[None, :],
        key_weight * column_scale[None, :],
        head_maxima,
    )


def solution(mesh):
    rows = P(("dp", "tensor"), None)
    by_column, by_row, by_dp = P("dp", "tensor"), P("tensor", "dp"), P("dp")
    up_spec, down_spec = P(None, "dp", "tensor"), P(None, "tensor", "dp")
    sizes = dict(mesh.shape)
    return jax.shard_map(
        functools.partial(body, sizes),
        mesh=mesh,
        in_specs=(
            rows, rows, by_column, by_column, by_column, by_row, by_dp, by_dp, up_spec, down_spec,
            by_dp, by_dp, P("dp", None), P("dp", None), P("tensor"),
        ),
        out_specs=(
            rows, rows, by_column, by_column, by_column, by_row, by_dp, by_dp, up_spec, down_spec,
            by_dp, by_dp, by_column, by_column, P("tensor"),
        ),
        check_vma=False,
    )
```

```python
import functools
import math

import jax
import jax.numpy as jnp
from jax import lax
from jax.experimental import pallas as pl
from jax.experimental.pallas import tpu as pltpu
from jax.sharding import PartitionSpec as P

HD = 64
SEQ = 197
CAP = 792
EPSILON = 1e-06
F32 = jnp.float32
BF16 = jnp.bfloat16
OUTER = 8
EXTRA = 16
ROW_TILE = 256
WINDOW = 256
MIB = 1 << 20


def up(number, unit):
    return -(-number // unit) * unit


def dot(left, right, contract=((1,), (0,))):
    return lax.dot_general(left, right, (contract, ((), ())), preferred_element_type=F32)


def params(mib):
    return pltpu.CompilerParams(vmem_limit_bytes=mib * MIB)


def any_spec():
    return pl.BlockSpec(memory_space=pl.ANY)


def vmem_spec():
    return pl.BlockSpec(memory_space=pltpu.VMEM)


def smem_spec():
    return pl.BlockSpec(memory_space=pltpu.SMEM)


def sds(shape, dtype):
    return jax.ShapeDtypeStruct(shape, dtype)


def cost(microseconds):
    return pl.CostEstimate(flops=int(microseconds * 0.5e9), bytes_accessed=0, transcendentals=0)


def after(value, *others):
    return lax.optimization_barrier((value, *others))[0]


def block_flip(x_bit, low_bit, high_bit):
    return x_bit | low_bit << 1 | high_bit << 2


def norm_stats(values):
    mean = jnp.mean(values, -1, keepdims=True)
    centred = values - mean
    scale = lax.rsqrt(jnp.mean(centred * centred, -1, keepdims=True) + EPSILON)
    return centred * scale, scale


def spread_rows(source, target, images, stride):
    for i in range(images):
        target[i * stride : i * stride + SEQ, :] = source[i * SEQ : (i + 1) * SEQ, :].astype(F32)
        end = (i + 1) * stride if i + 1 < images else target.shape[0]
        target[i * stride + SEQ : end, :] = jnp.zeros((end - i * stride - SEQ, target.shape[1]), F32)


def gather_rows(source, target, images, stride):
    for i in range(images):
        target[i * SEQ : (i + 1) * SEQ, :] = source[i * stride : i * stride + SEQ, :]


def attention_forward_kernel(images, stride, heads, layout, *refs):
    n_pieces = len(layout)
    place_ref, x_ref, gains_ref = refs[:3]
    piece_refs = refs[3 : 3 + n_pieces]
    res_ref, second_ref, first_ref, w_ref, kept_ref, peak_ref = refs[3 + n_pieces : 9 + n_pieces]
    scratch, sems = refs[9 + n_pieces :]
    columns = heads * HD
    block = w_ref.shape[1] // OUTER
    place = place_ref[0]
    copies = []
    for ref, entries in zip(piece_refs, layout):
        for j, (t, flip) in enumerate(entries):
            row = pl.multiple_of((place ^ flip) * block, 16)
            copies.append(
                pltpu.make_async_copy(
                    ref.at[j, pl.ds(0, block), :],
                    w_ref.at[t, pl.ds(row, block), :],
                    sems.at[len(copies)],
                )
            )
            copies[-1].start()
    spread_rows(x_ref, res_ref, images, stride)
    unit, _ = norm_stats(res_ref[...])
    first_ref[...] = (unit * gains_ref[0:1, :] + gains_ref[1:2, :]).astype(BF16)
    for copy in copies:
        copy.wait()
    scale = 1.0 / math.sqrt(HD)
    key_ok = lax.broadcasted_iota(jnp.int32, (stride, stride), 0) < SEQ
    query_ok = lax.broadcasted_iota(jnp.int32, (1, stride), 1) < SEQ
    lane = lax.broadcasted_iota(jnp.int32, (8, 128), 1)

    def step(t, carry):
        scratch[...] = dot(first_ref[...], w_ref[t]).astype(BF16).astype(F32)
        peaks = jnp.full((8, 128), -jnp.inf, F32)
        for i in range(images):
            rows = slice(i * stride, (i + 1) * stride)
            for h in range(heads):
                at = [slice((1 + p) * columns + h * HD, (1 + p) * columns + (h + 1) * HD) for p in range(3)]
                q = (scratch[rows, at[0]] * scale).astype(BF16)
                k = scratch[rows, at[1]].astype(BF16)
                v = scratch[rows, at[2]].astype(BF16)
                s = jnp.where(key_ok, dot(k, q, ((1,), (1,))), -1e30)
                top = jnp.max(s, 0, keepdims=True)
                e = jnp.exp(s - top)
                p = e * (1.0 / jnp.sum(e, 0, keepdims=True))
                o = dot(v, p.astype(BF16), ((0,), (0,))).T
                scratch[rows, h * HD : (h + 1) * HD] = o.astype(BF16).astype(F32)
                peak = jnp.max(jnp.where(query_ok, top, -jnp.inf), keepdims=True)
                peaks = jnp.maximum(peaks, jnp.where(lane == h, peak, -jnp.inf))
        peak_ref[t] = peaks
        kept_ref[t] = scratch[...].astype(BF16)
        res_ref[...] += dot(kept_ref[t, :, 0:columns], w_ref[t, :, 0:columns], ((1,), (1,)))
        return carry

    lax.fori_loop(0, w_ref.shape[0], step, 0)
    unit, _ = norm_stats(res_ref[...])
    second_ref[...] = (unit * gains_ref[2:3, :] + gains_ref[3:4, :]).astype(BF16)


def attention_forward(place, rows, gains, pieces, layout, images, stride, padded, parts, heads):
    features = rows.shape[1]
    n_copies = sum(len(entries) for entries in layout)
    return pl.pallas_call(
        functools.partial(attention_forward_kernel, images, stride, heads, layout),
        out_shape=(
            sds((padded, features), F32),
            sds((padded, features), BF16),
            sds((padded, features), BF16),
            sds((parts, features, features), BF16),
            sds((parts, padded, features), BF16),
            sds((parts, 8, 128), F32),
        ),
        in_specs=[smem_spec(), vmem_spec(), vmem_spec()] + [any_spec()] * len(pieces),
        out_specs=(vmem_spec(),) * 6,
        scratch_shapes=[
            pltpu.VMEM((padded, features), F32),
            pltpu.SemaphoreType.DMA((n_copies,)),
        ],
        compiler_params=params(48),
        cost_estimate=cost(22),
        name="attention_forward",
    )(place, rows, gains, *pieces)


def head_at(columns, part, head):
    return slice(part * columns + head * HD, part * columns + (head + 1) * HD)


def norm_back(grad, gain, unit, scale):
    weighted = grad * gain
    mean = jnp.mean(weighted, -1, keepdims=True)
    return (weighted - mean - unit * jnp.mean(weighted * unit, -1, keepdims=True)) * scale


def heads_backward(images, stride, heads, t, w_ref, kept_ref, half_ref, firsts, halves, kept, mixed, grads, total):
    columns = heads * HD
    features = w_ref.shape[2]
    scale = 1.0 / math.sqrt(HD)
    key_ok = lax.broadcasted_iota(jnp.int32, (stride, stride), 0) < SEQ
    kept[...] = kept_ref[t, 0].astype(F32)
    mixed[...] = dot(half_ref[...], w_ref[t, 0, :, 0:columns]).astype(BF16).astype(F32)
    for i in range(images):
        rows = slice(i * stride, (i + 1) * stride)
        for h in range(heads):
            q = (kept[rows, head_at(columns, 1, h)] * scale).astype(BF16)
            k = kept[rows, head_at(columns, 2, h)].astype(BF16)
            v = kept[rows, head_at(columns, 3, h)].astype(BF16)
            do = mixed[rows, h * HD : (h + 1) * HD].astype(BF16)
            s = jnp.where(key_ok, dot(k, q, ((1,), (1,))), -1e30)
            e = jnp.exp(s - jnp.max(s, 0, keepdims=True))
            p = e * (1.0 / jnp.sum(e, 0, keepdims=True))
            dp = dot(v, do, ((1,), (1,)))
            dv = dot(p.astype(BF16), do)
            ds = (p * (dp - jnp.sum(p * dp, 0, keepdims=True))).astype(BF16)
            dq = dot(k, ds, ((0,), (0,))).T * scale
            dk = dot(ds, q)
            grads[rows, head_at(columns, 1, h)] = dq
            grads[rows, head_at(columns, 2, h)] = dk
            grads[rows, head_at(columns, 3, h)] = dv
    packed = grads[...].astype(BF16)
    total[...] += dot(packed, w_ref[t, 0], ((1,), (1,)))
    full = dot(firsts[...], packed)
    out = dot(halves[...], kept_ref[t, 0, :, 0:columns])
    full = full + jnp.concatenate((out, jnp.zeros((features, features - columns), F32)), 1)
    return full.astype(BF16)


def half_spec(value, y):
    return pl.BlockSpec((2, 1) + value.shape[2:], lambda i: (0, y, 0, 0))


def put_blocks(refs, t, full):
    block = full.shape[0] // OUTER
    for i, ref in enumerate(refs):

        @pl.when(t == i)
        def _(ref=ref):
            for j in range(OUTER):
                ref[j, 0:block, :] = full[j * block : (j + 1) * block, :]


def attention_backward_kernel(images, stride, heads, *refs):
    (cot_ref, res_ref, d0_ref, d1_ref, d2_ref, first_ref, w_ref, kept_ref, gains_ref, extra_ref) = refs[:10]
    keep_ref, send_ref, resid, half, total, firsts, halves, more_ref = refs[10:18]
    kept, grads, mixed = refs[18:]
    features = w_ref.shape[2]
    unit, scale_two = norm_stats(res_ref[...])
    da2 = d0_ref[...].astype(F32) + d1_ref[...].astype(F32) + d2_ref[...].astype(F32)
    row = lax.broadcasted_iota(jnp.int32, (EXTRA, features), 0)
    extra = jnp.where(row == 2, jnp.sum(da2 * unit, 0, keepdims=True), extra_ref[...])
    more_ref[...] = jnp.where(row == 3, jnp.sum(da2, 0, keepdims=True), extra)
    spread_rows(cot_ref, resid, images, stride)
    resid[...] += norm_back(da2, gains_ref[2:3, :], unit, scale_two)
    half[...] = resid[...].astype(BF16)
    firsts[...] = first_ref[...].T
    halves[...] = half[...].T
    total[...] = jnp.zeros_like(total)
    grads[...] = jnp.zeros_like(grads)

    def step(t, carry):
        full = heads_backward(
            images, stride, heads, t, w_ref, kept_ref, half, firsts, halves, kept, mixed, grads, total
        )
        put_blocks((keep_ref, send_ref), t, full)
        return carry

    lax.fori_loop(0, 2, step, 0)


def attention_rest_kernel(images, stride, heads, *refs):
    (x_ref, resid_ref, half, total_ref, firsts, halves, w_ref, kept_ref, gains_ref, more_ref) = refs[:10]
    input_grad_ref, keep_ref, send_ref, extra_ref = refs[10:14]
    kept, grads, mixed, total = refs[14:]
    features = w_ref.shape[2]
    block = features // OUTER
    total[...] = total_ref[...]
    grads[...] = jnp.zeros_like(grads)

    def step(t, carry):
        full = heads_backward(
            images, stride, heads, t, w_ref, kept_ref, half, firsts, halves, kept, mixed, grads, total
        )
        put_blocks((keep_ref, send_ref), t, full)
        return carry

    lax.fori_loop(0, 2, step, 0)
    spread_rows(x_ref, kept, images, stride)
    unit, scale_one = norm_stats(kept[...])
    da = total[...]
    grads[...] = resid_ref[...] + norm_back(da, gains_ref[0:1, :], unit, scale_one)
    gather_rows(grads, input_grad_ref, images, stride)
    row = lax.broadcasted_iota(jnp.int32, (EXTRA, features), 0)
    extra = jnp.where(row == 0, jnp.sum(da * unit, 0, keepdims=True), more_ref[...])
    extra = jnp.where(row == 1, jnp.sum(da, 0, keepdims=True), extra).astype(BF16)
    extra_ref[...] = extra
    for ref in (keep_ref, send_ref):
        for j in range(OUTER):
            ref[j, block : block + EXTRA, :] = extra


def attention_backward(cot, residual, pieces, first, weights, kept, gains, extra, images, stride, heads):
    padded, features = first.shape
    share = sds((OUTER, features // OUTER, features), BF16)
    wide, half, turned = sds((padded, features), F32), sds((padded, features), BF16), sds((features, padded), BF16)
    return pl.pallas_call(
        functools.partial(attention_backward_kernel, images, stride, heads),
        grid=(1,),
        out_shape=(share, share, wide, half, wide, turned, turned, sds((EXTRA, features), F32)),
        in_specs=[vmem_spec()] * 6 + [half_spec(weights, 1), half_spec(kept, 1)] + [vmem_spec()] * 2,
        out_specs=(vmem_spec(),) * 8,
        scratch_shapes=[
            pltpu.VMEM((padded, features), F32),
            pltpu.VMEM((padded, features), F32),
            pltpu.VMEM((padded, heads * HD), F32),
        ],
        compiler_params=params(50),
        cost_estimate=cost(20),
        name="attention_backward",
    )(cot, residual, *pieces, first, weights, kept, gains, extra)


def attention_rest(rows, resid, half, total, firsts, halves, weights, kept, gains, more, images, stride, heads):
    padded, features = resid.shape
    share = sds((OUTER, features // OUTER + EXTRA, features), BF16)
    return pl.pallas_call(
        functools.partial(attention_rest_kernel, images, stride, heads),
        grid=(1,),
        out_shape=(sds(rows.shape, F32), share, share, sds((EXTRA, features), BF16)),
        in_specs=[vmem_spec()] * 6 + [half_spec(weights, 0), half_spec(kept, 0)] + [vmem_spec()] * 2,
        out_specs=(vmem_spec(),) * 4,
        scratch_shapes=[
            pltpu.VMEM((padded, features), F32),
            pltpu.VMEM((padded, features), F32),
            pltpu.VMEM((padded, heads * HD), F32),
            pltpu.VMEM((padded, features), F32),
        ],
        compiler_params=params(50),
        cost_estimate=cost(20),
        name="attention_backward_rest",
    )(rows, resid, half, total, firsts, halves, weights, kept, gains, more)


def dispatch_kernel(gated, *refs):
    table_ref = refs[0]
    slot_ref = refs[-3] if gated else refs[-2]
    gate_ref = refs[-2] if gated else None
    out_ref = refs[-1]
    shard_refs = []
    for ref in refs[1 : -3 if gated else -2]:
        shard_refs += [ref] if len(ref.shape) == 2 else [ref.at[i] for i in range(ref.shape[0])]
    n_shards = len(shard_refs)
    expert = pl.program_id(0)
    experts = pl.num_programs(0)
    padded = shard_refs[0].shape[0]
    features = shard_refs[0].shape[1]
    count_all = table_ref[2 * n_shards * experts + expert]
    tail = pl.multiple_of(count_all // 16 * 16, 16)
    out_ref[0, pl.ds(tail, ROW_TILE + 16), :] = jnp.zeros((ROW_TILE + 16, features), BF16)
    row16 = lax.broadcasted_iota(jnp.int32, (16, 1), 0)
    rows = lax.broadcasted_iota(jnp.int32, (WINDOW, padded), 0)
    starts = [table_ref[expert * n_shards + r] for r in range(n_shards)]
    numbers = [table_ref[n_shards * experts + expert * n_shards + r] for r in range(n_shards)]
    firsts = [start // 16 * 16 for start in starts]
    steps = [
        (start - first + number + WINDOW - 1) // WINDOW
        for start, first, number in zip(starts, firsts, numbers)
    ]

    def step(r, c):
        low = pl.multiple_of(firsts[r] + c * WINDOW, 16)
        hit = slot_ref[0, r : r + 1, :] - low == rows
        chosen = jnp.where(hit, 1.0, 0.0)
        got = dot(chosen.astype(BF16), shard_refs[r][...])
        if gated:
            got = got * jnp.sum(chosen * gate_ref[0, r : r + 1, :], -1, keepdims=True)
        got = got.astype(BF16)
        before = out_ref[0, pl.ds(low, 16), :]
        out_ref[0, pl.ds(low, 16), :] = jnp.where(row16 + low < starts[r], before, got[:16])
        out_ref[0, pl.ds(low + 16, WINDOW - 16), :] = got[16:]

    short = functools.reduce(jnp.maximum, steps) <= 1

    @pl.when(short)
    def _():
        for r in range(n_shards):
            step(r, 0)

    @pl.when(jnp.logical_not(short))
    def _():
        for r in range(n_shards):

            def again(c, carry, r=r):
                step(r, c)
                return carry

            lax.fori_loop(0, steps[r], again, 0)


def slot_rows(limit):
    return up(limit, ROW_TILE) + WINDOW + 16


def dispatch(table, shards, slots, gates, limit):
    experts = slots.shape[0]
    padded, features = shards[0].shape[-2:]
    length = slot_rows(limit)
    gated = gates is not None
    per_expert = pl.BlockSpec((1,) + slots.shape[1:], lambda e: (e, 0, 0))
    return pl.pallas_call(
        functools.partial(dispatch_kernel, gated),
        grid=(experts,),
        out_shape=sds((experts, length, features), BF16),
        in_specs=[smem_spec()] + [vmem_spec()] * len(shards) + [per_expert] * (2 if gated else 1),
        out_specs=pl.BlockSpec((1, length, features), lambda e: (e, 0, 0)),
        compiler_params=params(48),
        cost_estimate=cost(15),
        name="dispatch_gated" if gated else "dispatch",
    )(table, *shards, slots, *([gates] if gated else []))


def normal_share(u):
    bell = jnp.exp(-0.5 * u * u)
    t = 1.0 / (1.0 + jnp.abs(u) * (0.3275911 / math.sqrt(2.0)))
    poly = 0.5 * 1.061405429
    for term in (-1.453152027, 1.421413741, -0.284496736, 0.254829592):
        poly = poly * t + 0.5 * term
    tail = poly * t * bell
    return jnp.where(u < 0, tail, 1.0 - tail), bell


def expert_kernel(*refs):
    info_ref, x_ref, dy_ref = refs[:3]
    w_refs = refs[3:11]
    y_ref, dx_ref = refs[11:13]
    share_refs = (refs[13:15], refs[15:17])
    w_in, w_out, g_in, g_out, hidden, slopes = refs[17:]
    place = info_ref[0]
    count = info_ref[1 + pl.program_id(0)]
    features = w_in.shape[0]
    block = features // OUTER
    for number, ref in enumerate(w_refs):
        flip = block_flip(number >> 2, number & 1, number >> 1 & 1)
        row = pl.multiple_of((place ^ flip) * block, 16)
        w_in[pl.ds(row, block), :] = ref[0, 0]
        w_out[pl.ds(row, block), :] = ref[0, 1]
    g_in[...] = jnp.zeros_like(g_in)
    g_out[...] = jnp.zeros_like(g_out)
    tiles = jnp.maximum((count + ROW_TILE - 1) // ROW_TILE, 1)

    def at(i):
        return pl.ds(pl.multiple_of(i * ROW_TILE, ROW_TILE), ROW_TILE)

    def first_half(i):
        pre = dot(x_ref[0, at(i), :], w_in[...])
        dh = dot(dy_ref[0, at(i), :], w_out[...])
        share, bell = normal_share(pre)
        hidden[i % 2] = (pre * share).astype(BF16)
        slope = share + pre * bell * (1.0 / math.sqrt(2.0 * math.pi))
        slopes[i % 2] = (dh * slope).astype(BF16)

    def second_half(i):
        hid, dpre = hidden[i % 2], slopes[i % 2]
        y_ref[0, at(i), :] = dot(hid, w_out[...], ((1,), (1,))).astype(BF16)
        dx_ref[0, at(i), :] = dot(dpre, w_in[...], ((1,), (1,))).astype(BF16)
        g_in[...] += dot(x_ref[0, at(i), :], dpre, ((0,), (0,)))
        g_out[...] += dot(dy_ref[0, at(i), :], hid, ((0,), (0,)))

    def tile(i, carry):
        second_half(i - 1)
        first_half(i)
        return carry

    first_half(0)
    lax.fori_loop(1, tiles, tile, 0)
    second_half(tiles - 1)
    rest = pl.ds(pl.multiple_of(tiles * ROW_TILE, 16), WINDOW + 16)
    y_ref[0, rest, :] = jnp.zeros((WINDOW + 16, features), BF16)
    dx_ref[0, rest, :] = jnp.zeros((WINDOW + 16, features), BF16)
    for number in range(OUTER):
        flip = block_flip(number >> 2 & 1, number & 1, number >> 1 & 1)
        row = pl.multiple_of((place ^ flip) * block, 16)
        in_ref, out_ref = share_refs[number // (OUTER // 2)]
        at = slice(number % (OUTER // 2) * block, (number % (OUTER // 2) + 1) * block)
        in_ref[0, at, :] = g_in[pl.ds(row, block), :].astype(BF16)
        out_ref[0, at, :] = g_out[pl.ds(row, block), :].astype(BF16)


def expert_math(info, x, dy, weights, first, experts, limit):
    length, features = x.shape[1:]
    hidden = weights[0].shape[3]
    most = up(limit, ROW_TILE)
    slots_spec = pl.BlockSpec((1, most, features), lambda e: (e + first, 0, 0))
    out_spec = pl.BlockSpec((1, length, features), lambda e: (e, 0, 0))
    share = sds((experts, features // 2, hidden), BF16)
    share_spec = pl.BlockSpec((1, features // 2, hidden), lambda e: (e, 0, 0))
    return pl.pallas_call(
        expert_kernel,
        grid=(experts,),
        out_shape=(sds((experts, length, features), BF16),) * 2 + (share,) * 4,
        in_specs=[smem_spec(), slots_spec, slots_spec]
        + [pl.BlockSpec((1,) + w.shape[1:], lambda e, at=first * (w.shape[0] > experts): (e + at, 0, 0, 0))
            for w in weights
],
        out_specs=(out_spec, out_spec) + (share_spec,) * 4,
        scratch_shapes=[
            pltpu.VMEM((features, hidden), BF16),
            pltpu.VMEM((features, hidden), BF16),
            pltpu.VMEM((features, hidden), F32),
            pltpu.VMEM((features, hidden), F32),
            pltpu.VMEM((2, ROW_TILE, hidden), BF16),
            pltpu.VMEM((2, ROW_TILE, hidden), BF16),
        ],
        compiler_params=params(60),
        cost_estimate=cost(33),
        name="expert_math",
    )(info, x, dy, *weights)


def combine_kernel(gated, n_sources, *refs):
    table_ref = refs[0]
    source_refs = refs[1 : 1 + n_sources]
    slot_ref = refs[1 + n_sources]
    gate_ref = refs[2 + n_sources] if gated else None
    send_ref, keep_ref, window = refs[-3:]
    r = pl.program_id(0)
    n_shards = pl.num_programs(0)
    per_source = source_refs[0].shape[0]
    experts = per_source * n_sources
    shard = lax.rem(r + n_shards // 2, n_shards)
    padded = slot_ref.shape[1]
    lanes = lax.broadcasted_iota(jnp.int32, (padded, WINDOW), 1)

    def chosen(e, low):
        hit = slot_ref[0, :, e : e + 1] == lanes + low
        return jnp.where(hit, gate_ref[0, :, e : e + 1] if gated else 1.0, 0.0).astype(BF16)

    firsts, steps, parts = [], [], []
    for e in range(experts):
        start = table_ref[e * n_shards + shard]
        number = table_ref[n_shards * experts + e * n_shards + shard]
        first = pl.multiple_of(start // 16 * 16, 16)
        firsts.append(first)
        steps.append((start - first + number + WINDOW - 1) // WINDOW)
        window[e * WINDOW : (e + 1) * WINDOW, :] = source_refs[e // per_source][e % per_source, pl.ds(first, WINDOW), :]
        parts.append(chosen(e, first))
    middle = padded // 32 * 16
    total = jnp.concatenate(
        [
            dot(jnp.concatenate([part[rows] for part in parts], 1), window[...]).astype(BF16)
            for rows in (slice(0, middle), slice(middle, padded))
        ],
        0,
    )

    def finish(ref):
        ref[0] = total
        for e in range(experts):

            def step(c, carry, e=e):
                low = pl.multiple_of(firsts[e] + c * WINDOW, 16)
                rows = source_refs[e // per_source][e % per_source, pl.ds(low, WINDOW), :]
                ref[0] = (ref[0].astype(F32) + dot(chosen(e, low), rows)).astype(BF16)
                return carry

            lax.fori_loop(1, steps[e], step, 0)

    @pl.when(r < n_shards // 2)
    def _():
        finish(send_ref)

    @pl.when(r >= n_shards // 2)
    def _():
        finish(keep_ref)


def combine(table, sources, slots, gates):
    n_shards, padded, experts = slots.shape
    features = sources[0].shape[2]
    gated = gates is not None
    half = n_shards // 2
    per_shard = pl.BlockSpec((1, padded, experts), lambda r: (lax.rem(r + half, n_shards), 0, 0))
    share = sds((half, padded, features), BF16)
    return pl.pallas_call(
        functools.partial(combine_kernel, gated, len(sources)),
        grid=(n_shards,),
        out_shape=(share, share),
        in_specs=[smem_spec()] + [vmem_spec()] * len(sources) + [per_shard] * (2 if gated else 1),
        out_specs=(
            pl.BlockSpec((1, padded, features), lambda r: (jnp.minimum(r, half - 1), 0, 0)),
            pl.BlockSpec((1, padded, features), lambda r: (jnp.maximum(r - half, 0), 0, 0)),
        ),
        scratch_shapes=[pltpu.VMEM((experts * WINDOW, features), BF16)],
        compiler_params=params(48),
        cost_estimate=cost(2),
        name="combine_gated" if gated else "combine",
    )(table, *sources, slots, *([gates] if gated else []))


def spread_kernel(images, stride, x_ref, out_ref, scratch):
    spread_rows(x_ref, scratch, images, stride)
    out_ref[...] = scratch[...].astype(BF16)


def spread(rows, images, stride, padded):
    return pl.pallas_call(
        functools.partial(spread_kernel, images, stride),
        out_shape=sds((padded, rows.shape[1]), BF16),
        in_specs=[vmem_spec()],
        out_specs=vmem_spec(),
        scratch_shapes=[pltpu.VMEM((padded, rows.shape[1]), F32)],
        compiler_params=params(16),
        cost_estimate=cost(2),
        name="spread_rows",
    )(rows)


def finish_kernel(images, stride, res_ref, a_ref, b_ref, c_ref, out_ref, scratch):
    mixture = a_ref[...].astype(F32) + b_ref[...].astype(F32) + c_ref[...].astype(F32)
    scratch[...] = res_ref[...] + mixture
    gather_rows(scratch, out_ref, images, stride)


def finish(residual, pieces, tokens, images, stride):
    return pl.pallas_call(
        functools.partial(finish_kernel, images, stride),
        out_shape=sds((tokens, residual.shape[1]), F32),
        in_specs=[vmem_spec()] * 4,
        out_specs=vmem_spec(),
        scratch_shapes=[pltpu.VMEM(residual.shape, F32)],
        compiler_params=params(24),
        cost_estimate=cost(2),
        name="finish_rows",
    )(residual, *pieces)


def body(
    sizes,
    block_input,
    cotangent,
    query_weight,
    key_weight,
    value_weight,
    output_weight,
    first_gain,
    first_shift,
    expert_in,
    expert_out,
    second_gain,
    second_shift,
    routes,
    route_gates,
    clip_threshold,
):
    dp, tensor = sizes["dp"], sizes["tensor"]
    inner = dp // OUTER
    tokens, features = block_input.shape
    columns = query_weight.shape[1]
    heads = columns // HD
    images = tokens // SEQ
    stride = up(SEQ, 8)
    padded = up(images * stride, 16)
    experts = expert_in.shape[0]
    mine = experts // 2
    half = mine // 2
    block = features // OUTER
    limit = 2 * CAP
    dp_at = lax.axis_index("dp")
    place = dp_at // inner
    tensor_at = lax.axis_index("tensor")
    low_bit = place >> 1 & 1

    def along(axis, size, flip):
        pairs = [(i, i ^ flip) for i in range(size)]
        return lambda value: lax.ppermute(value, axis, pairs)

    send_x = along("dp", dp, 1 * inner)
    send_low = along("dp", dp, 2 * inner)
    send_high = along("dp", dp, 4 * inner)
    send_core = along("tensor", tensor, 1)
    send_y = along("tensor", tensor, 2)

    def whole_block(value, axis):
        if inner == 1:
            return value
        every = lax.all_gather(value, "dp", axis=axis, tiled=True)
        return lax.dynamic_slice_in_dim(every, place * block, block, axis)

    def own_rows(value, axis):
        if inner == 1:
            return value
        shape = list(value.shape)
        shape[axis] = features
        every = lax.dynamic_update_slice_in_dim(jnp.zeros(shape, value.dtype), value, place * block, axis)
        return lax.psum_scatter(every, "dp", scatter_dimension=axis, tiled=True)

    packed = jnp.concatenate(
        (output_weight.T, query_weight, key_weight, value_weight), 1
    ).astype(BF16)
    packed = whole_block(packed, 0)
    norms = jnp.stack((first_gain, first_shift, second_gain, second_shift)).astype(BF16)
    norms = whole_block(norms, 1)
    norms = lax.dynamic_update_slice(jnp.zeros((EXTRA, features), BF16), norms, (0, place * block))
    own = jnp.concatenate((packed, norms), 0)[None]
    cot_half = spread(cotangent, images, stride, padded)
    cot_y = send_y(cot_half)
    pair = jnp.concatenate((own, send_high(own)), 0)
    four = jnp.concatenate((pair, send_low(pair)), 0)
    four_x, four_y = send_x(four), send_y(four)
    cot_low = send_low(after(cot_half, four))

    w_in = whole_block(expert_in.astype(BF16), 1)
    w_out = whole_block(expert_out.astype(BF16), 2).swapaxes(1, 2)
    both = jnp.stack((w_in, w_out), 1)
    w_keep = lax.dynamic_slice_in_dim(both, low_bit * mine, mine, 0)
    w_give = lax.dynamic_slice_in_dim(both, (1 - low_bit) * mine, mine, 0)
    w_high_first = send_high(after(w_keep[:1], four))
    w_high_rest = send_high(after(w_keep[1:3], w_high_first))

    eight = jnp.concatenate((four, four_x), 0)
    two_a, two_b = send_x(after(four_y[:2], w_high_first)), send_y(four_x[2:])
    eight_y = after(jnp.concatenate((four_y, two_a, two_b), 0), cot_low)
    pieces = [eight, eight_y, send_core(eight), send_core(eight_y)]
    flips = tuple(block_flip(x_bit, low, high) for x_bit in (0, 1) for low in (0, 1) for high in (0, 1))
    layout = [tuple((t, flip) for flip in flips) for t in range(4)]
    gains = jnp.sum(eight[:, block:].astype(F32), 0)
    w_low = send_low(after(w_give, cot_low))
    cot_far = send_y(cot_low)
    w_keep_x = send_x(after(w_keep, two_a))

    table = jnp.concatenate((routes.T.astype(F32), route_gates.T), 0)
    picks = routes.shape[1]
    table = table.reshape(2 * picks, tensor, images, SEQ)
    table = jnp.pad(table, ((0, 0), (0, 0), (0, 0), (0, stride - SEQ)), constant_values=-1)
    table = table.reshape(2 * picks, tensor, images * stride)
    table = jnp.pad(table, ((0, 0), (0, 0), (0, padded - images * stride)), constant_values=-1)
    table = jnp.stack((table, send_low(table)))
    table = table.reshape(2, 2 * picks, 2, 2, padded)
    table = jnp.where(tensor_at >> 1 & 1 == 1, table[:, :, ::-1], table)
    table = jnp.where(tensor_at & 1 == 1, table[:, :, :, ::-1], table)
    table = table.transpose(1, 3, 0, 2, 4).reshape(2 * picks, 8, padded)
    ids = (low_bit * mine + jnp.arange(mine)).astype(F32)[None, :, None, None]
    hits = table[:picks, None] == ids
    chosen = jnp.any(hits, 0)
    gates = jnp.sum(jnp.where(hits, table[picks:, None], 0.0), 0)
    order = lax.broadcasted_iota(jnp.int32, (padded, padded), 0) < lax.broadcasted_iota(
        jnp.int32, (padded, padded), 1
    )
    before = jnp.dot(
        chosen.reshape(-1, padded).astype(BF16), order.astype(BF16), preferred_element_type=F32
    ).reshape(chosen.shape)
    counts = jnp.sum(chosen.astype(F32), -1)
    ahead = (jnp.arange(8)[:, None] < jnp.arange(8)[None, :]).astype(F32)
    starts = jnp.sum(counts[:, :, None] * ahead[None], 1)
    slots = jnp.where(chosen, starts[:, :, None] + before, -1.0).astype(jnp.int32)
    totals = jnp.sum(counts, 1)
    scalars = jnp.concatenate((starts.reshape(-1), counts.reshape(-1), totals)).astype(jnp.int32)
    slot_columns = slots.transpose(1, 2, 0)
    gate_columns = gates.transpose(1, 2, 0)

    place_word = place.astype(jnp.int32).reshape(1)
    residual, second, first, weights, kept, peaks = attention_forward(
        after(place_word, scalars, slots, gates, slot_columns, gate_columns), block_input, gains, pieces, layout, images, stride, padded, tensor, heads
    )
    second, w_low, w_high_rest, w_keep_x, cot_far = lax.optimization_barrier(
        (second, w_low, w_high_rest, w_keep_x, cot_far)
    )
    w_high_last = send_high(after(w_keep[3:], w_high_rest))

    by_low, by_y = send_low(second), send_y(second)
    w_low_x = send_x(w_low)
    cot_shards = jnp.stack((cot_half, cot_y, cot_low, cot_far))
    cot_slots = dispatch(scalars, (cot_shards, send_core(cot_shards)), slots, gates, limit)
    w_low_0 = send_high(after(w_low[:half], second))
    cot_slots, by_low, by_y, w_low_x, w_high_last = lax.optimization_barrier(
        (cot_slots, by_low, by_y, w_low_x, w_high_last)
    )
    w_high = jnp.concatenate((w_high_first, w_high_rest, w_high_last), 0)
    by_far = send_y(by_low)
    shards = [second, by_y, by_low, by_far]
    shards += [send_core(piece) for piece in shards]
    w_high_x = send_x(after(w_high, w_low_x))
    w_low_1 = send_high(after(w_low[half:], by_low))
    w_low_x_0 = send_x(after(w_low_0, w_high_x))
    x_slots = dispatch(after(scalars, w_low_0), shards, slots, None, limit)
    w_low_1 = after(w_low_1, x_slots)
    w_low_x_1 = send_x(w_low_1)

    def run_experts(c, x, weights):
        info = jnp.concatenate((place_word, totals[c * half : (c + 1) * half].astype(jnp.int32)))
        return expert_math(info, x, cot_slots, weights, c * half, half, limit)

    basic = (w_keep, w_low, w_high)
    basic_x = (w_keep_x, w_low_x, w_high_x)
    y_0, dx_0, *shares_0 = run_experts(0, after(x_slots, w_low_1), (*basic, w_low_0, *basic_x, w_low_x_0))
    keep_0, give_0 = shares_0[:2], shares_0[2:]
    give_0[0], x_slots = lax.optimization_barrier((give_0[0], x_slots, w_low_x_1))[:2]
    side_in_0 = send_x(give_0[0])
    y_1, dx_1, *shares_1 = run_experts(1, x_slots, (*basic, w_low_1, *basic_x, w_low_x_1))
    keep_1, give_1 = shares_1[:2], shares_1[2:]
    dx_1 = after(dx_1, side_in_0)
    side_out_0 = send_x(after(give_0[1], dx_1))
    rows = keep_0[0].shape[1] // 2

    def upper_sum(keep, side):
        return keep[:, rows:] + side[:, rows:]

    def lower_sum(keep, side, high):
        return (keep[:, :rows].astype(F32) + side[:, :rows].astype(F32) + high.astype(F32)).astype(BF16)

    high_in_0 = send_high(after(upper_sum(keep_0[0], side_in_0), dx_1))
    give, hold = combine(scalars, (dx_0, dx_1), slot_columns, None)
    give, side_out_0, high_in_0 = lax.optimization_barrier((give, side_out_0, high_in_0))
    core = send_core(give)
    high_out_0 = send_high(after(upper_sum(keep_0[1], side_out_0), give))
    sums = [hold[i] + core[i] for i in range(4)]
    far_y, near_y = send_y(sums[3]), send_y(sums[1])
    side_in_1 = send_x(after(give_1[0], give))
    give, hold_y = combine(after(scalars, sums[3]), (y_0, y_1), slot_columns, gate_columns)
    give, side_in_1, far_y, high_out_0 = lax.optimization_barrier((give, side_in_1, far_y, high_out_0))
    core_y = send_core(give)
    low = send_low(sums[2] + far_y)
    side_out_1 = send_x(after(give_1[1], give))
    mixture = [hold_y[i] + core_y[i] for i in range(4)]
    mixture_y = send_y(jnp.stack((mixture[1], mixture[3])))
    high_in_1 = send_high(after(upper_sum(keep_1[0], side_in_1), high_out_0))
    high_out_1 = send_high(after(upper_sum(keep_1[1], side_out_1), high_out_0))
    grad_pieces = (after(sums[0], *mixture), near_y, low)
    mine_0 = jnp.stack(
        (lower_sum(keep_0[0], side_in_0, high_in_0), lower_sum(keep_0[1], side_out_0, high_out_0)), 1
    )
    low_0 = send_low(mine_0[:, :, block:])

    peak = peaks[:, 0, :heads].reshape(2, 2, heads)
    peak = jnp.where(tensor_at & 1 == 1, peak[::-1], peak)
    peak = jnp.where(tensor_at >> 1 & 1 == 1, peak[:, ::-1], peak)
    peak = peak.transpose(1, 0, 2).reshape(tensor * heads)
    extra = jnp.zeros((EXTRA, features), F32)
    if inner == 1:
        device = dp_at * tensor + tensor_at
        high = lax.reduce_precision(peak, 8, 7)
        rest = lax.reduce_precision(peak - high, 8, 7)
        is_mine = (jnp.arange(dp * tensor) == device)[None, :, None]
        words = jnp.where(is_mine, jnp.stack((high, rest))[:, None, :], 0.0).reshape(2, -1)
        extra = extra.at[4:6, : words.shape[1]].set(words)
    weights = weights.reshape(2, 2, features, features)
    kept = kept.reshape(2, 2, padded, features)
    keep_b, send_b, resid, dattn, total, firsts, halves, extra = attention_backward(
        cotangent, residual, grad_pieces, first, weights, kept, gains, extra, images, stride, heads
    )
    total, send_b, mixture_y, high_in_1, low_0, side_out_1 = lax.optimization_barrier(
        (total, send_b, mixture_y, high_in_1, low_0, side_out_1)
    )
    upper = send_y(keep_b + send_core(send_b))
    mixture_low = send_low(mixture[2] + mixture_y[1])
    input_grad, keep, send, extra = attention_rest(
        block_input, resid, dattn, total, firsts, halves, weights, kept, gains, extra, images, stride, heads
    )
    send, extra, upper, high_out_1, mixture_low = lax.optimization_barrier(
        (send, extra, upper, high_out_1, mixture_low)
    )
    mine_1 = jnp.stack(
        (lower_sum(keep_1[0], side_in_1, high_in_1), lower_sum(keep_1[1], side_out_1, high_out_1)), 1
    )
    low_1 = send_low(mine_1[:, :, block:])

    near = send_core(send)
    extra_y = send_y(extra)
    extra_far = lax.ppermute(extra, "tensor", [(i, i ^ 3) for i in range(tensor)])
    others = jnp.broadcast_to(extra_y.astype(F32) + extra_far.astype(F32), (OUTER, EXTRA, features))
    others = jnp.concatenate((upper.astype(F32), others), 1)
    total = (keep.astype(F32) + near.astype(F32) + others).astype(BF16)
    block_output = finish(residual, (mixture[0], mixture_y[0], mixture_low), tokens, images, stride)

    own_share = jnp.concatenate((mine_0[:, :, :block], mine_1[:, :, :block]), 0)
    far_share = jnp.concatenate((low_0, low_1), 0)
    grads = jnp.concatenate(
        (
            jnp.where(low_bit == 0, own_share, far_share),
            jnp.where(low_bit == 0, far_share, own_share),
        ),
        0,
    ).astype(F32)
    expert_in_grad = own_rows(grads[:, 0], 1)
    expert_out_grad = own_rows(grads[:, 1].swapaxes(1, 2), 2)

    if inner == 1:
        total = lax.all_to_all(total, "dp", 0, 0, tiled=True)
        total = jnp.sum(total.astype(F32), 0)
        words = total[block:]
        total = total[:block]
        peak = jnp.sum(words[4:6, : dp * tensor * tensor * heads], 0).reshape(dp * tensor, tensor * heads)
        peak = jnp.max(peak, 0)
    else:
        words = lax.psum(total[0, block:].astype(F32), "dp")
        total = total[:, :block].reshape(features, features).astype(F32)
        total = lax.psum_scatter(total, "dp", scatter_dimension=0, tiled=True)
        peak = lax.pmax(peak, ("dp", "tensor"))
    head_maxima = lax.dynamic_slice_in_dim(peak, tensor_at * heads, heads, 0)
    vectors = lax.dynamic_slice_in_dim(words[:4], dp_at * (features // dp), features // dp, 1)
    output_grad, query_grad, key_grad, value_grad = (
        total[:, i * columns : (i + 1) * columns] for i in range(4)
    )
    factor = jnp.minimum(1.0, clip_threshold / jnp.maximum(head_maxima, 1.0))
    column_scale = jnp.repeat(jnp.sqrt(factor), HD)
    return (
        block_output,
        input_grad,
        query_grad,
        key_grad,
        value_grad,
        output_grad.T,
        vectors[0],
        vectors[1],
        expert_in_grad,
        expert_out_grad,
        vectors[2],
        vectors[3],
        query_weight * column_scale[None, :],
        key_weight * column_scale[None, :],
        head_maxima,
    )


def solution(mesh):
    rows = P(("dp", "tensor"), None)
    by_column, by_row, by_dp = P("dp", "tensor"), P("tensor", "dp"), P("dp")
    up_spec, down_spec = P(None, "dp", "tensor"), P(None, "tensor", "dp")
    sizes = dict(mesh.shape)
    return jax.shard_map(
        functools.partial(body, sizes),
        mesh=mesh,
        in_specs=(
            rows, rows, by_column, by_column, by_column, by_row, by_dp, by_dp, up_spec, down_spec,
            by_dp, by_dp, P("dp", None), P("dp", None), P("tensor"),
        ),
        out_specs=(
            rows, rows, by_column, by_column, by_column, by_row, by_dp, by_dp, up_spec, down_spec,
            by_dp, by_dp, by_column, by_column, P("tensor"),
        ),
        check_vma=False,
    )
```
